256 devices in a mesh: dp: 8 (over z), cls: 32 (over y, x, core).
Axes of the slice: x: 4, y: 4, z: 8, core: 2. Of those that a mesh axis runs over, the one named last changes fastest.
Arguments:
- weak_embed: bfloat16 [512, 512], P('dp'), may hold values from -6 to 6
- strong_embed: bfloat16 [512, 512], P('dp'), may hold values from -0.0625 to 0.0625
- centers: bfloat16 [1048576, 512], P(('dp', 'cls')), may hold values from -0.0625 to 0.0625
- marginal: float32 [1048576], P(('dp', 'cls')), may hold values from 0.25 to 45
- pseudo_label: int32 [512], P('dp'), may hold values from 0 to 1048575
- confident: int32 [512], P('dp'), may hold values 0 or 1
Outputs:
- new_marginal: float32 [1048576], P(('dp', 'cls'))
- center_grad: bfloat16 [1048576, 512], P(('dp', 'cls'))
- embed_grad: float32 [512, 512], P('dp')
- loss: float32 [], replicated
The draws below stay inside these ranges and needn't reach their ends.
All inputs are finite; a program needn't handle non-finite values. No bound on the sum of `confident` on one device may be relied on, other than what follows from the above.
Results may differ from the reference program's by a relative error of at most 0.00155.
The reference program's roundings to bfloat16 on the way count: a program that leaves them out, or rounds other values in their place, can miss the bound.
Values may be sent and summed in bfloat16 or wider, within the bound.
A program may use at most 128 MiB of HBM per device.

```python
import jax
import jax.numpy as jnp
from jax import lax

D = 512
IMG = 64
ROWS = 512
CLASSES = 1048576
N_DP = 8


def draw_marginal(key, part):
    key = jax.random.fold_in(key, 11)
    place = jnp.arange(CLASSES, dtype=jnp.float32) / CLASSES
    ramp = jnp.exp(place * jnp.log(10.0))
    jitter = jnp.exp(jax.random.uniform(key, (CLASSES,), jnp.float32, jnp.log(0.5), jnp.log(2.0)))
    return (ramp * jitter).astype(jnp.float32)


def with_ends(drawn, own_key, least, largest):
    extent = drawn.shape
    spot = [jax.random.randint(jax.random.fold_in(own_key, axis), (), 0, extent[axis]) for axis in range(len(extent))]
    drawn = drawn.at[tuple(spot)].set(least)
    longest = extent.index(max(extent))
    spot[longest] = (spot[longest] + 1) % extent[longest]
    return drawn.at[tuple(spot)].set(largest)


def levels(rng, shape, split, least, high):
    factor_of = 1.0
    for axis_at, blocks in split:
        draws = jax.random.uniform(jax.random.fold_in(jax.random.fold_in(rng, 6), axis_at), (blocks,), jnp.float32, least / len(split), high / len(split))
        factor_of = factor_of * jnp.repeat(jnp.exp(draws), shape[axis_at] // blocks).reshape((-1,) + (1,) * (len(shape) - 1 - axis_at))
    return factor_of


def gaussian(own_key, extent, scale, limit, shards=(), kind=jnp.bfloat16):
    loudness = levels(own_key, extent, shards, -0.22, 0.18) if shards else 1.0
    array = jax.random.normal(own_key, extent, jnp.float32) * scale * loudness
    return jnp.minimum(jnp.maximum(array, -limit), limit).astype(kind)


def setup_inputs(seed: int = 0) -> dict:
    seeds = jax.random.split(jax.random.key(seed), 7)
    return {
        "weak_embed": gaussian(seeds[0], (ROWS, D), 1.0, 6.0, ((0, 8),)),
        "strong_embed": gaussian(seeds[1], (ROWS, D), 0.004, 0.0625, ((0, 8),)),
        "centers": gaussian(seeds[2], (CLASSES, D), 0.004, 0.0625, ((0, 256),)),
        "marginal": draw_marginal(jax.random.fold_in(seeds[6], 71), 0),
        "pseudo_label": with_ends(jax.random.randint(seeds[4], (ROWS,), 0, CLASSES), jax.random.fold_in(seeds[4], 1), 0, CLASSES - 1).astype(jnp.int32),
        "confident": with_ends((jax.random.randint(seeds[5], (ROWS,), 0, 4) < 3).astype(jnp.int32), jax.random.fold_in(seeds[5], 1), 0, 1),
    }


SCALE = 64.0
MARGIN = 0.35
MOMENTUM = 0.9
EPS = 1e-06

def unit_rows(values):
    exact = values.astype(jnp.float32)
    inverse = lax.rsqrt(lax.optimization_barrier(jnp.sum(exact * exact, axis=-1, keepdims=True)) + EPS)
    return (exact * inverse, inverse)

def reference(weak_embed, strong_embed, centers, marginal, pseudo_label, confident):
    weak_exact, _ = unit_rows(weak_embed)
    weak_unit = weak_exact.astype(jnp.bfloat16)
    strong_exact, strong_inv = unit_rows(strong_embed)
    strong_unit = strong_exact.astype(jnp.bfloat16)
    flags = confident.astype(jnp.float32)
    block = CLASSES // N_DP
    blocks = centers.reshape(N_DP, block, D)
    marg_blocks = marginal.reshape(N_DP, block)
    offsets = jnp.arange(N_DP, dtype=jnp.int32) * block

    def prepare(cblock, offset):
        center_exact, center_inv = unit_rows(cblock)
        center_unit = center_exact.astype(jnp.bfloat16)
        teach = jnp.exp(SCALE * (jnp.dot(weak_unit, center_unit.T, preferred_element_type=jnp.float32) - 1.0))
        ids = offset + jnp.arange(block, dtype=jnp.int32)
        hit = (pseudo_label[:, None] == ids[None, :]).astype(jnp.float32)
        stud = SCALE * (jnp.dot(strong_unit, center_unit.T, preferred_element_type=jnp.float32) - MARGIN * hit)
        return (center_exact, center_inv, center_unit, teach, stud, hit)

    def first(items):
        cblock, offset = items
        _, _, _, teach, stud, hit = prepare(cblock, offset)
        return (lax.optimization_barrier(jnp.sum(teach, axis=1)), lax.optimization_barrier(jnp.sum(jnp.exp(stud - SCALE), axis=1)), lax.optimization_barrier(jnp.sum(hit * stud, axis=1)))
    zparts, yparts, lparts = lax.map(first, (blocks, offsets))
    teacher_total = lax.optimization_barrier(jnp.sum(zparts, axis=0))
    student_total = lax.optimization_barrier(jnp.sum(yparts, axis=0))
    label_logit = lax.optimization_barrier(jnp.sum(lparts, axis=0))

    def second(items):
        cblock, offset, mblock = items
        _, _, _, teach, stud, hit = prepare(cblock, offset)
        share = teach / teacher_total[:, None]
        batch = CLASSES / ROWS * lax.optimization_barrier(jnp.sum(share, axis=0))
        fresh = MOMENTUM * mblock + (1.0 - MOMENTUM) * batch
        raw = share / fresh[None, :]
        return (fresh, lax.optimization_barrier(jnp.sum(raw, axis=1)), lax.optimization_barrier(jnp.sum(raw * stud, axis=1)))
    fresh_blocks, qparts, rparts = lax.map(second, (blocks, offsets, marg_blocks))
    aligned_total = lax.optimization_barrier(jnp.sum(qparts, axis=0))
    aligned_cross = lax.optimization_barrier(jnp.sum(rparts, axis=0))
    loss = jnp.sum(flags * (SCALE + jnp.log(student_total) - 0.5 * label_logit - 0.5 * aligned_cross / aligned_total)) / IMG

    def third(items):
        cblock, offset, fresh = items
        center_exact, center_inv, center_unit, teach, stud, hit = prepare(cblock, offset)
        raw = teach / teacher_total[:, None] / fresh[None, :]
        grad = SCALE / IMG * flags[:, None] * (jnp.exp(stud - SCALE) / student_total[:, None] - 0.5 * hit - 0.5 * raw / aligned_total[:, None])
        grad = grad.astype(jnp.bfloat16)
        unit_part = jnp.dot(grad, center_unit, preferred_element_type=jnp.float32)
        cgrad = jnp.dot(grad.T, strong_unit, preferred_element_type=jnp.float32)
        cgrad = (cgrad - center_exact * lax.optimization_barrier(jnp.sum(center_exact * cgrad, axis=1, keepdims=True))) * center_inv
        return (unit_part, cgrad.astype(jnp.bfloat16))
    unit_parts, cgrads = lax.map(third, (blocks, offsets, fresh_blocks))
    unit_grad = lax.optimization_barrier(jnp.sum(unit_parts, axis=0))
    embed_grad = (unit_grad - strong_exact * lax.optimization_barrier(jnp.sum(strong_exact * unit_grad, axis=1, keepdims=True))) * strong_inv
    return (fresh_blocks.reshape(CLASSES), cgrads.reshape(CLASSES, D), embed_grad, loss)
```

```python
import functools
import math

import jax
import jax.numpy as jnp
from jax import lax
from jax.experimental import pallas as pl
from jax.experimental.pallas import tpu as pltpu
from jax.sharding import PartitionSpec as P

SCALE = 64.0
MARGIN = 0.35
MOMENTUM = 0.9
EPS = 1e-06
LOG2 = SCALE * math.log2(math.e)
MESH = pl.DeviceIdType.MESH
F32 = jnp.float32
BF16 = jnp.bfloat16
CH = 256
LANES = 128


def unit_rows(values):
    exact = values.astype(F32)
    inverse = lax.rsqrt(jnp.sum(exact * exact, axis=-1, keepdims=True) + EPS)
    return exact * inverse, inverse


def nt(a, b):
    return lax.dot_general(a, b, (((1,), (1,)), ((), ())), preferred_element_type=F32)


def kernel(
    nz, ncls,
    weak_hbm, strong_hbm, centers_hbm, marginal_hbm, label_hbm, flag_hbm,
    fresh_out, cgrad_out, egrad_out, loss_out,
    weak_own, strong_own, ints_own, marg,
    weak_all, strong_all, ints_all, label_row, flag_row,
    c_raw, c_unit, c_unit_t, c_inv, marg_col,
    teach, stud_dot, stud_exp, grad_t,
    vec_t, vec_q, vec_e,
    msg_a, msg_b, got_a, got_b,
    part_l, part_r, half_buf, half_got, plane_got, z_send, z_got, tile_own, tile_got,
    in_sem, c_sem,
    ring_send, ring_recv, sib_send, sib_recv, int_send, int_recv,
    a_send, a_recv, b_send, b_recv,
    half_send, half_recv, plane_send, plane_recv, z_send_sem, z_recv_sem, tile_send, tile_recv,
):
    img = weak_own.shape[0]
    half = img // 2
    classes = c_raw.shape[0]
    rows = weak_all.shape[0]
    width = weak_all.shape[1]
    blocks = rows // LANES
    nplane = ncls // 2
    z = lax.axis_index("dp")
    cls = lax.axis_index("cls")
    core = lax.rem(cls, 2)
    plane = lax.div(cls, 2)
    sibling = cls + 1 - 2 * core

    quarter = classes // 4
    own_copies = [
        pltpu.make_async_copy(weak_hbm, weak_own, in_sem.at[0]),
        pltpu.make_async_copy(strong_hbm, strong_own, in_sem.at[1]),
        pltpu.make_async_copy(label_hbm, ints_own.at[pl.ds(0, 1)], in_sem.at[2]),
        pltpu.make_async_copy(flag_hbm, ints_own.at[pl.ds(1, 1)], in_sem.at[3]),
        pltpu.make_async_copy(marginal_hbm, marg, in_sem.at[4]),
    ]
    for copy in own_copies:
        copy.start()
    c_copies = [
        pltpu.make_async_copy(
            centers_hbm.at[pl.ds(q * quarter, quarter)], c_raw.at[pl.ds(q * quarter, quarter)], c_sem.at[q]
        )
        for q in range(4)
    ]
    for copy in c_copies:
        copy.start()

    barrier = pltpu.get_barrier_semaphore()

    def greet_z(k, carry):
        pl.semaphore_signal(barrier, inc=1, device_id={"dp": lax.rem(z + k, nz)}, device_id_type=MESH)
        return carry

    def greet_cls(k, carry):
        pl.semaphore_signal(barrier, inc=1, device_id={"cls": lax.rem(cls + k, ncls)}, device_id_type=MESH)
        return carry

    lax.fori_loop(1, nz, greet_z, 0)
    lax.fori_loop(1, ncls, greet_cls, 0)

    own_copies[0].wait()
    own_copies[1].wait()
    base = pl.multiple_of(z * img, img)
    weak_exact, _ = unit_rows(weak_own[...])
    weak_all[pl.ds(base, img), :] = weak_exact.astype(BF16)
    strong_exact, strong_inv = unit_rows(strong_own[...])
    strong_all[pl.ds(base, img), :] = strong_exact.astype(BF16)
    own_copies[2].wait()
    own_copies[3].wait()
    mine = ints_own[:, 0:img]
    both = jnp.concatenate([mine, mine], axis=1)
    lane = lax.broadcasted_iota(jnp.int32, both.shape, 1)
    ints_all[z] = jnp.where(lax.div(lane, img) == lax.rem(z, 2), both, 0)

    pl.semaphore_wait(barrier, nz - 1 + ncls - 1)

    views = (weak_all, strong_all)
    hops = [(nz // 2, nz - 1 - nz // 2), (nz - 1 - nz // 2, nz // 2)]

    def piece(view, block):
        return views[view].at[pl.ds(pl.multiple_of(block * img + core * half, half), half)]

    def ring_copy(view, way, step):
        block = lax.rem(z - step + nz, nz) if way == 0 else lax.rem(z + step, nz)
        to = lax.rem(z + 1, nz) if way == 0 else lax.rem(z + nz - 1, nz)
        ref = piece(view, block)
        return pltpu.make_async_remote_copy(
            ref, ref, ring_send.at[view, way, step], ring_recv.at[view, way, step],
            device_id={"dp": to}, device_id_type=MESH,
        )

    def sib_copy(view, block):
        ref = piece(view, block)
        return pltpu.make_async_remote_copy(
            ref, ref, sib_send.at[view], sib_recv.at[view], device_id={"cls": sibling}, device_id_type=MESH
        )

    for view in range(2):
        for way in range(2):
            ring_copy(view, way, 0).start()

    def int_copy(k, carry):
        pltpu.make_async_remote_copy(
            ints_all.at[z], ints_all.at[z], int_send, int_recv,
            device_id={"dp": lax.rem(z + k, nz)}, device_id_type=MESH,
        ).start()
        return carry

    lax.fori_loop(1, nz, int_copy, 0)

    def ring_step(view, step):
        for way in range(2):
            if step >= hops[view][way]:
                continue
            ring_copy(view, way, step).wait_recv()
            if step + 1 < hops[view][way]:
                ring_copy(view, way, step + 1).start()
            block = lax.rem(z - 1 - step + nz, nz) if way == 0 else lax.rem(z + 1 + step, nz)
            sib_copy(view, block).start()

    eye = lax.broadcasted_iota(jnp.int32, (LANES, LANES), 0) == lax.broadcasted_iota(jnp.int32, (LANES, LANES), 1)

    def prepare(q):
        c_copies[q].wait()

        def step(i, carry):
            at = pl.ds(pl.multiple_of(i * CH, CH), CH)
            exact, inv = unit_rows(c_raw[at, :])
            c_unit[at, :] = (exact * 1.0).astype(BF16)
            c_inv[at, :] = jnp.broadcast_to(inv, (CH, LANES))
            return carry

        lax.fori_loop(q * quarter // CH, (q + 1) * quarter // CH, step, 0)

    def transpose_units(q):
        def step(i, carry):
            at = pl.ds(pl.multiple_of(i * CH, CH), CH)
            c_unit_t[:, at] = c_unit[at, :].T
            return carry

        lax.fori_loop(q * quarter // CH, (q + 1) * quarter // CH, step, 0)

    def marginal_columns():
        own_copies[4].wait()

        def step(j, carry):
            row = jnp.broadcast_to(marg[pl.ds(j, 1), :], (LANES, LANES))
            column = jnp.sum(jnp.where(eye, row, 0.0), axis=1, keepdims=True)
            marg_col[pl.ds(pl.multiple_of(j * LANES, LANES), LANES), :] = jnp.broadcast_to(column, (LANES, LANES))
            return carry

        lax.fori_loop(0, classes // LANES, step, 0)

    steps = nz // 2
    for s in range(max(steps, 4)):
        if s < 4:
            prepare(s)
        if s < steps:
            for view in range(2):
                ring_step(view, s)
        if s == 0:
            marginal_columns()

    pltpu.make_async_copy(ints_all.at[pl.ds(0, nz - 1)], ints_all.at[pl.ds(0, nz - 1)], int_recv).wait()
    pltpu.make_async_copy(ints_all.at[pl.ds(0, nz - 1)], ints_all.at[pl.ds(0, nz - 1)], int_send).wait()
    offset = (z * ncls + cls) * classes
    for j in range(blocks):
        pair = ints_all[2 * j] + ints_all[2 * j + 1]
        label_row[0:1, j * LANES : (j + 1) * LANES] = pair[0:1, :] - offset
        flag_row[0:1, j * LANES : (j + 1) * LANES] = pair[1:2, :].astype(F32)

    def sib_wait(view):
        whole = views[view].at[pl.ds(0, (nz - 1) * half)]
        pltpu.make_async_copy(whole, whole, sib_recv.at[view]).wait()

    def a_start(n):
        def go(k, carry):
            pltpu.make_async_remote_copy(
                msg_a.at[n], got_a.at[n, cls], a_send.at[n], a_recv.at[n],
                device_id={"cls": lax.rem(cls + k, ncls)}, device_id_type=MESH,
            ).start()
            return carry

        got_a[n, cls] = msg_a[n]
        lax.fori_loop(1, ncls, go, 0)

    def b_start(n):
        whole = got_a.at[n, pl.ds(0, ncls - 1)]
        pltpu.make_async_copy(whole, whole, a_recv.at[n]).wait()
        total = jnp.sum(got_a[n], axis=0)
        msg_b[n] = total
        got_b[n, z] = total

        def go(k, carry):
            pltpu.make_async_remote_copy(
                msg_b.at[n], got_b.at[n, z], b_send.at[n], b_recv.at[n],
                device_id={"dp": lax.rem(z + k, nz)}, device_id_type=MESH,
            ).start()
            return carry

        lax.fori_loop(1, nz, go, 0)

    def b_finish(n):
        whole = got_b.at[n, pl.ds(0, nz - 1)]
        pltpu.make_async_copy(whole, whole, b_recv.at[n]).wait()
        return jnp.sum(got_b[n], axis=0)

    def to_blocks(row, ref, n):
        for j in range(blocks):
            ref[n, j : j + 1, :] = row[:, j * LANES : (j + 1) * LANES]

    def to_row(block, ref):
        for j in range(blocks):
            ref[0:1, j * LANES : (j + 1) * LANES] = block[j : j + 1, :]

    def fold(value):
        return jnp.sum(value.reshape(value.shape[0] // 8, 8, value.shape[1]), axis=0)

    def span(i):
        return pl.ds(pl.multiple_of(i * CH, CH), CH)

    def hits(i):
        ids = lax.broadcasted_iota(jnp.int32, (CH, rows), 0) + i * CH
        return ids == label_row[...]

    n_chunks = classes // CH
    zero = jnp.zeros((8, rows), F32)

    sib_wait(0)

    def teacher_step(i, total):
        at = span(i)
        value = jnp.exp2(nt(c_unit[at, :], weak_all[...]) * LOG2 - LOG2)
        teach[at, :] = value
        return total + fold(value)

    total = lax.fori_loop(0, n_chunks, teacher_step, zero, unroll=2)
    to_blocks(jnp.sum(total, axis=0, keepdims=True), msg_a, 0)
    a_start(0)

    sib_wait(1)

    def student_step(i, carry):
        total, label_dot = carry
        at = span(i)
        hit = hits(i)
        dot = nt(c_unit[at, :], strong_all[...])
        dot = jnp.where(hit, dot - MARGIN, dot)
        stud_dot[at, :] = dot
        value = jnp.exp2(dot * LOG2 - LOG2)
        stud_exp[at, :] = value
        return total + fold(value), label_dot + fold(jnp.where(hit, dot, 0.0))

    carry = lax.fori_loop(0, n_chunks // 2, student_step, (zero, zero), unroll=2)
    b_start(0)
    total, label_dot = lax.fori_loop(n_chunks // 2, n_chunks, student_step, carry, unroll=2)
    to_blocks(jnp.sum(total, axis=0, keepdims=True), msg_a, 1)
    a_start(1)
    to_blocks(SCALE * jnp.sum(label_dot, axis=0, keepdims=True), part_l, 0)
    to_row(1.0 / b_finish(0), vec_t)

    per_row = float(classes * nz * ncls) / rows

    def aligned_step(i, carry):
        q_total, r_total = carry
        at = span(i)
        share = teach[at, :] * vec_t[...]
        batch = per_row * jnp.sum(share, axis=1, keepdims=True)
        fresh = MOMENTUM * marg_col[at, :] + (1.0 - MOMENTUM) * batch
        for j in range(CH // LANES):
            part = fresh[j * LANES : (j + 1) * LANES, :]
            fresh_out[pl.ds(i * (CH // LANES) + j, 1), :] = jnp.sum(jnp.where(eye, part, 0.0), axis=0, keepdims=True)
        inverse = 1.0 / fresh
        raw = share * jnp.concatenate([inverse] * blocks, axis=1)
        teach[at, :] = raw
        return q_total + fold(raw), r_total + fold(raw * stud_dot[at, :])

    carry = lax.fori_loop(0, n_chunks // 2, aligned_step, (zero, zero))
    b_start(1)
    q_total, r_total = lax.fori_loop(n_chunks // 2, n_chunks, aligned_step, carry)
    to_blocks(jnp.sum(q_total, axis=0, keepdims=True), msg_a, 2)
    a_start(2)
    to_blocks(SCALE * jnp.sum(r_total, axis=0, keepdims=True), part_r, 0)
    transpose_units(0)
    transpose_units(1)
    student_total = b_finish(1)
    b_start(2)
    transpose_units(2)
    transpose_units(3)
    aligned_total = b_finish(2)

    to_row(1.0 / student_total, vec_e)
    to_row(-0.5 / aligned_total, vec_q)
    vec_e[...] = vec_e[...] * flag_row[...]
    vec_q[...] = vec_q[...] * flag_row[...]

    def grad_step(i, carry):
        at = span(i)
        value = stud_exp[at, :] * vec_e[...] + teach[at, :] * vec_q[...]
        value = jnp.where(hits(i), value - 0.5 * flag_row[...], value)
        grad_t[at, :] = value.astype(BF16)
        return carry

    lax.fori_loop(0, n_chunks, grad_step, 0, unroll=2)

    flags_block = jnp.concatenate(
        [flag_row[0:1, j * LANES : (j + 1) * LANES] for j in range(blocks)], axis=0
    )
    loss_part = flags_block * (-0.5 * part_l[0] - 0.5 * part_r[0] / aligned_total)
    loss_tile = jnp.concatenate([loss_part, jnp.zeros((8 - blocks, LANES), F32)], axis=0)
    tile_rows = img // 8
    tile_cols = width // 2 // LANES
    per = tile_rows * tile_cols // nplane

    def unit_half(which):
        at = pl.ds(pl.multiple_of(which * (width // 2), width // 2), width // 2)
        out = jnp.dot(c_unit_t[at, :], grad_t[...], preferred_element_type=F32).T
        for block in range(nz):
            for t in range(tile_rows):
                for c in range(tile_cols):
                    index = t * tile_cols + c
                    row = block * img + t * 8
                    half_buf[which, index // per, block * per + index % per] = out[
                        row : row + 8, c * LANES : (c + 1) * LANES
                    ]
        for p in range(nplane):
            half_buf[which, p, nz * per] = loss_tile

    unit_half(1 - core)
    half_copy = pltpu.make_async_remote_copy(
        half_buf.at[1 - core], half_got, half_send, half_recv, device_id={"cls": sibling}, device_id_type=MESH
    )
    half_copy.start()
    unit_half(core)
    half_copy.wait()

    def half_add(p, carry):
        half_buf[core, p] = half_buf[core, p] + half_got[p]
        return carry

    lax.fori_loop(0, nplane, half_add, 0)

    def plane_copy(k, carry):
        p = lax.rem(plane + k, nplane)
        pltpu.make_async_remote_copy(
            half_buf.at[core, p], plane_got.at[plane], plane_send, plane_recv,
            device_id={"cls": p * 2 + core}, device_id_type=MESH,
        ).start()
        return carry

    lax.fori_loop(1, nplane, plane_copy, 0)
    plane_got[plane] = half_buf[core, plane]

    def center_step(i, carry):
        at = span(i)
        value = jnp.dot(grad_t[at, :], strong_all[...], preferred_element_type=F32)
        inverse = jnp.concatenate([c_inv[at, :]] * (width // LANES), axis=1)
        exact = c_raw[at, :].astype(F32) * inverse
        along = jnp.sum(exact * value, axis=1, keepdims=True)
        cgrad_out[at, :] = ((value - exact * along) * inverse).astype(BF16)
        return carry

    third = n_chunks * 5 // 8
    lax.fori_loop(0, third, center_step, 0, unroll=2)

    whole = plane_got.at[pl.ds(0, nplane - 1)]
    pltpu.make_async_copy(whole, whole, plane_recv).wait()
    plane_sum = jnp.sum(plane_got[...], axis=0)
    for block in range(nz):
        z_send[block, 0:per] = plane_sum[block * per : (block + 1) * per]
        z_send[block, per] = plane_sum[nz * per]
    z_got[z] = z_send[z]

    def z_copy(k, carry):
        to = lax.rem(z + k, nz)
        pltpu.make_async_remote_copy(
            z_send.at[to], z_got.at[z], z_send_sem, z_recv_sem, device_id={"dp": to}, device_id_type=MESH
        ).start()
        return carry

    lax.fori_loop(1, nz, z_copy, 0)

    two = n_chunks * 7 // 8
    lax.fori_loop(third, two, center_step, 0, unroll=2)

    whole_z = z_got.at[pl.ds(0, nz - 1)]
    pltpu.make_async_copy(whole_z, whole_z, z_recv_sem).wait()
    z_sum = jnp.sum(z_got[...], axis=0)
    tile_own[...] = z_sum[0:per]
    tile_got[cls] = z_sum[0:per]

    def tile_copy(k, carry):
        pltpu.make_async_remote_copy(
            tile_own, tile_got.at[cls], tile_send, tile_recv,
            device_id={"cls": lax.rem(cls + k, ncls)}, device_id_type=MESH,
        ).start()
        return carry

    lax.fori_loop(1, ncls, tile_copy, 0)

    lax.fori_loop(two, n_chunks, center_step, 0, unroll=2)

    loss_rows = flags_block * (SCALE + jnp.log(student_total)) + z_sum[per, 0:blocks, :]
    loss_out[...] = jnp.sum(jnp.sum(loss_rows, axis=1, keepdims=True), axis=0, keepdims=True) / img

    whole_t = tile_got.at[pl.ds(0, ncls - 1)]
    pltpu.make_async_copy(whole_t, whole_t, tile_recv).wait()
    bands = []
    for t in range(tile_rows):
        tiles = []
        for c in range(2 * tile_cols):
            index = t * tile_cols + c % tile_cols
            tiles.append(tile_got[(index // per) * 2 + c // tile_cols, index % per])
        bands.append(jnp.concatenate(tiles, axis=1))
    unit_grad = jnp.concatenate(bands, axis=0)
    exact, inverse = unit_rows(strong_own[...])
    egrad_out[...] = (unit_grad - exact * jnp.sum(exact * unit_grad, axis=1, keepdims=True)) * inverse

    for view in range(2):
        for way in range(2):
            for step in range(hops[view][way]):
                ring_copy(view, way, step).wait_send()
        sent = views[view].at[pl.ds(0, (nz - 1) * half)]
        pltpu.make_async_copy(sent, sent, sib_send.at[view]).wait()
    for n in range(3):
        sent = got_a.at[n, pl.ds(0, ncls - 1)]
        pltpu.make_async_copy(sent, sent, a_send.at[n]).wait()
        sent = got_b.at[n, pl.ds(0, nz - 1)]
        pltpu.make_async_copy(sent, sent, b_send.at[n]).wait()
    pltpu.make_async_copy(whole, whole, plane_send).wait()
    pltpu.make_async_copy(whole_z, whole_z, z_send_sem).wait()
    pltpu.make_async_copy(whole_t, whole_t, tile_send).wait()


def body(nz, ncls, weak_embed, strong_embed, centers, marginal, pseudo_label, confident):
    img, width = weak_embed.shape
    classes = centers.shape[0]
    rows = img * nz
    blocks = rows // LANES
    nplane = ncls // 2
    per = (img // 8) * (width // 2 // LANES) // nplane
    vmem = pltpu.VMEM
    dma = pltpu.SemaphoreType.DMA
    hop = nz // 2
    scratch = [
        vmem((img, width), BF16), vmem((img, width), BF16), vmem((2, img), jnp.int32), vmem((classes // LANES, LANES), F32),
        vmem((rows, width), BF16), vmem((rows, width), BF16), vmem((nz, 2, LANES), jnp.int32),
        vmem((1, rows), jnp.int32), vmem((1, rows), F32),
        vmem((classes, width), BF16), vmem((classes, width), BF16), vmem((width, classes), BF16),
        vmem((classes, LANES), F32), vmem((classes, LANES), F32),
        vmem((classes, rows), F32), vmem((classes, rows), F32), vmem((classes, rows), F32), vmem((classes, rows), BF16),
        vmem((1, rows), F32), vmem((1, rows), F32), vmem((1, rows), F32),
        vmem((3, blocks, LANES), F32), vmem((3, blocks, LANES), F32),
        vmem((3, ncls, blocks, LANES), F32), vmem((3, nz, blocks, LANES), F32),
        vmem((1, blocks, LANES), F32), vmem((1, blocks, LANES), F32),
        vmem((2, nplane, nz * per + 1, 8, LANES), F32), vmem((nplane, nz * per + 1, 8, LANES), F32),
        vmem((nplane, nz * per + 1, 8, LANES), F32),
        vmem((nz, per + 1, 8, LANES), F32), vmem((nz, per + 1, 8, LANES), F32),
        vmem((per, 8, LANES), F32), vmem((ncls, per, 8, LANES), F32),
        dma((5,)), dma((4,)),
        dma((2, 2, hop)), dma((2, 2, hop)), dma((2,)), dma((2,)), dma, dma,
        dma((3,)), dma((3,)), dma((3,)), dma((3,)),
        dma, dma, dma, dma, dma, dma, dma, dma,
    ]
    hbm = pl.BlockSpec(memory_space=pl.ANY)
    local = pl.BlockSpec(memory_space=pltpu.VMEM)
    fresh, cgrad, egrad, loss = pl.pallas_call(
        functools.partial(kernel, nz, ncls),
        out_shape=(
            jax.ShapeDtypeStruct((classes // LANES, LANES), F32),
            jax.ShapeDtypeStruct((classes, width), BF16),
            jax.ShapeDtypeStruct((img, width), F32),
            jax.ShapeDtypeStruct((1, 1), F32),
        ),
        in_specs=[hbm] * 6,
        out_specs=(local,) * 4,
        scratch_shapes=scratch,
        compiler_params=pltpu.CompilerParams(
            collective_id=0, has_side_effects=True, vmem_limit_bytes=55 * 1024 * 1024
        ),
    )(
        weak_embed, strong_embed, centers, marginal.reshape(classes // LANES, LANES),
        pseudo_label.reshape(1, img), confident.reshape(1, img),
    )
    return fresh.reshape(classes), cgrad, egrad, loss.reshape(())


def solution(mesh):
    placed = (
        P("dp", None),
        P("dp", None),
        P(("dp", "cls"), None),
        P(("dp", "cls")),
        P("dp"),
        P("dp"),
    )
    return jax.shard_map(
        functools.partial(body, mesh.shape["dp"], mesh.shape["cls"]),
        mesh=mesh,
        in_specs=placed,
        out_specs=(P(("dp", "cls")), P(("dp", "cls"), None), P("dp", None), P()),
        check_vma=False,
    )
```

```python
import functools
import math

import jax
import jax.numpy as jnp
from jax import lax
from jax.experimental import pallas as pl
from jax.experimental.pallas import tpu as pltpu
from jax.sharding import PartitionSpec as P

SCALE = 64.0
MARGIN = 0.35
MOMENTUM = 0.9
EPS = 1e-06
LOG2 = SCALE * math.log2(math.e)
MESH = pl.DeviceIdType.MESH
F32 = jnp.float32
BF16 = jnp.bfloat16
CH = 256
TCH, TUN = 256, 4
SCH, SUN = 256, 4
LANES = 128


def unit_rows(values):
    exact = values.astype(F32)
    inverse = lax.rsqrt(jnp.sum(exact * exact, axis=-1, keepdims=True) + EPS)
    return exact * inverse, inverse


def nt(a, b):
    return lax.dot_general(a, b, (((1,), (1,)), ((), ())), preferred_element_type=F32)


def kernel(
    nz, ncls,
    weak_hbm, strong_hbm, centers_hbm, marginal_hbm, label_hbm, flag_hbm,
    fresh_out, cgrad_out, egrad_out, loss_out,
    weak_own, strong_own, ints_own, marg,
    weak_all, strong_all, ints_all, label_row, flag_row,
    c_raw, c_unit, c_unit_t, c_inv, marg_col,
    teach, stud_dot, stud_exp, grad_t,
    vec_t, vec_q, vec_e,
    msg_a, msg_b, got_a, got_b,
    part_l, part_r, half_buf, half_got, plane_got, z_send, z_got, tile_own, tile_got,
    in_sem, c_sem,
    gather_send, gather_recv, sib_send, sib_recv, int_send, int_recv,
    a_send, a_recv, b_send, b_recv,
    half_send, half_recv, plane_send, plane_recv, z_send_sem, z_recv_sem, tile_send, tile_recv,
):
    img = weak_own.shape[0]
    half = img // 2
    classes = c_raw.shape[0]
    rows = weak_all.shape[0]
    width = weak_all.shape[1]
    blocks = rows // LANES
    nplane = ncls // 2
    z = lax.axis_index("dp")
    cls = lax.axis_index("cls")
    core = lax.rem(cls, 2)
    plane = lax.div(cls, 2)
    sibling = cls + 1 - 2 * core

    quarter = classes // 4
    own_copies = [
        pltpu.make_async_copy(weak_hbm, weak_own, in_sem.at[0]),
        pltpu.make_async_copy(strong_hbm, strong_own, in_sem.at[1]),
        pltpu.make_async_copy(label_hbm, ints_own.at[pl.ds(0, 1)], in_sem.at[2]),
        pltpu.make_async_copy(flag_hbm, ints_own.at[pl.ds(1, 1)], in_sem.at[3]),
        pltpu.make_async_copy(marginal_hbm, marg, in_sem.at[4]),
    ]
    for copy in own_copies:
        copy.start()
    c_copies = [
        pltpu.make_async_copy(
            centers_hbm.at[pl.ds(q * quarter, quarter)], c_raw.at[pl.ds(q * quarter, quarter)], c_sem.at[q]
        )
        for q in range(4)
    ]
    for copy in c_copies:
        copy.start()

    barrier = pltpu.get_barrier_semaphore()

    def greet_z(k, carry):
        pl.semaphore_signal(barrier, inc=1, device_id={"dp": lax.rem(z + k, nz)}, device_id_type=MESH)
        return carry

    def greet_cls(k, carry):
        pl.semaphore_signal(barrier, inc=1, device_id={"cls": lax.rem(cls + k, ncls)}, device_id_type=MESH)
        return carry

    lax.fori_loop(1, nz, greet_z, 0)
    lax.fori_loop(1, ncls, greet_cls, 0)
    base = pl.multiple_of(z * img, img)
    own_copies[0].wait()
    weak_exact, _ = unit_rows(weak_own[...])
    weak_all[pl.ds(base, img), :] = weak_exact.astype(BF16)
    pl.semaphore_wait(barrier, nz - 1 + ncls - 1)

    views = (weak_all, strong_all)
    near = nz // 2
    group, seat = lax.div(z, near), lax.rem(z, near)
    sends = [(away, k) for away in range(2) for k in range(near) if away or k]

    def piece(view, block):
        return views[view].at[pl.ds(pl.multiple_of(block * img + core * half, half), half)]

    def gather_copy(view, away, k):
        ref = piece(view, z)
        to = lax.rem(group + away, 2) * near + lax.rem(seat + k, near)
        at = away * near + k
        return pltpu.make_async_remote_copy(
            ref, ref, gather_send.at[view, at], gather_recv.at[view, at],
            device_id={"dp": to}, device_id_type=MESH,
        )

    def sib_copy(view, away, k):
        ref = piece(view, lax.rem(group + away, 2) * near + lax.rem(seat + near - k, near))
        return pltpu.make_async_remote_copy(
            ref, ref, sib_send.at[view, away], sib_recv.at[view, away],
            device_id={"cls": sibling}, device_id_type=MESH,
        )

    def int_copy(k, carry):
        pltpu.make_async_remote_copy(
            ints_all.at[z], ints_all.at[z], int_send, int_recv,
            device_id={"dp": lax.rem(z + k, nz)}, device_id_type=MESH,
        ).start()
        return carry

    for away, k in sends:
        gather_copy(0, away, k).start()
    own_copies[1].wait()
    strong_exact, _ = unit_rows(strong_own[...])
    strong_all[pl.ds(base, img), :] = strong_exact.astype(BF16)
    for away, k in sends:
        gather_copy(1, away, k).start()
    own_copies[2].wait()
    own_copies[3].wait()
    mine = ints_own[:, 0:img]
    both = jnp.concatenate([mine, mine], axis=1)
    lane = lax.broadcasted_iota(jnp.int32, both.shape, 1)
    ints_all[z] = jnp.where(lax.div(lane, img) == lax.rem(z, 2), both, 0)
    lax.fori_loop(1, nz, int_copy, 0)

    def pass_on(view, away):
        for k in range(near):
            if away or k:
                gather_copy(view, away, k).wait_recv()
                sib_copy(view, away, k).start()

    def sib_whole(view, away):
        return views[view].at[pl.ds(0, (near if away else near - 1) * half)]

    def sib_wait(view, away):
        whole = sib_whole(view, away)
        pltpu.make_async_copy(whole, whole, sib_recv.at[view, away]).wait()

    eye = lax.broadcasted_iota(jnp.int32, (LANES, LANES), 0) == lax.broadcasted_iota(jnp.int32, (LANES, LANES), 1)

    def prepare(q):
        c_copies[q].wait()

        def step(i, carry):
            at = pl.ds(pl.multiple_of(i * CH, CH), CH)
            exact, inv = unit_rows(c_raw[at, :])
            c_unit[at, :] = (exact * 1.0).astype(BF16)
            c_inv[at, :] = jnp.broadcast_to(inv, (CH, LANES))
            return carry

        lax.fori_loop(q * quarter // CH, (q + 1) * quarter // CH, step, 0)

    def transpose_units(q):
        def step(i, carry):
            at = pl.ds(pl.multiple_of(i * CH, CH), CH)
            c_unit_t[:, at] = c_unit[at, :].T
            return carry

        lax.fori_loop(q * quarter // CH, (q + 1) * quarter // CH, step, 0)

    def marginal_columns():
        own_copies[4].wait()

        def step(j, carry):
            row = jnp.broadcast_to(marg[pl.ds(j, 1), :], (LANES, LANES))
            column = jnp.sum(jnp.where(eye, row, 0.0), axis=1, keepdims=True)
            marg_col[pl.ds(pl.multiple_of(j * LANES, LANES), LANES), :] = jnp.broadcast_to(column, (LANES, LANES))
            return carry

        lax.fori_loop(0, classes // LANES, step, 0)

    for q in range(4):
        prepare(q)
    marginal_columns()

    def a_start(n):
        def go(k, carry):
            pltpu.make_async_remote_copy(
                msg_a.at[n], got_a.at[n, cls], a_send.at[n], a_recv.at[n],
                device_id={"cls": lax.rem(cls + k, ncls)}, device_id_type=MESH,
            ).start()
            return carry

        got_a[n, cls] = msg_a[n]
        lax.fori_loop(1, ncls, go, 0)

    def b_start(n):
        whole = got_a.at[n, pl.ds(0, ncls - 1)]
        pltpu.make_async_copy(whole, whole, a_recv.at[n]).wait()
        total = jnp.sum(got_a[n], axis=0)
        msg_b[n] = total
        got_b[n, z] = total

        def go(k, carry):
            pltpu.make_async_remote_copy(
                msg_b.at[n], got_b.at[n, z], b_send.at[n], b_recv.at[n],
                device_id={"dp": lax.rem(z + k, nz)}, device_id_type=MESH,
            ).start()
            return carry

        lax.fori_loop(1, nz, go, 0)

    def b_finish(n):
        whole = got_b.at[n, pl.ds(0, nz - 1)]
        pltpu.make_async_copy(whole, whole, b_recv.at[n]).wait()
        return jnp.sum(got_b[n], axis=0)

    def to_blocks(row, ref, n):
        for j in range(blocks):
            ref[n, j : j + 1, :] = row[:, j * LANES : (j + 1) * LANES]

    def to_row(block, ref):
        for j in range(blocks):
            ref[0:1, j * LANES : (j + 1) * LANES] = block[j : j + 1, :]

    def fold(value):
        return jnp.sum(value.reshape(value.shape[0] // 8, 8, value.shape[1]), axis=0)

    def span(i, size=CH):
        return pl.ds(pl.multiple_of(i * size, size), size)

    def hits(i, size=CH):
        ids = lax.broadcasted_iota(jnp.int32, (size, rows), 0) + i * size
        return ids == label_row[...]

    n_chunks = classes // CH
    zero = jnp.zeros((8, rows), F32)

    group_rows = rows // 2

    for away in range(2):
        pass_on(0, away)
        sib_wait(0, away)
        lanes = pl.ds(pl.multiple_of(lax.rem(group + away, 2) * group_rows, group_rows), group_rows)

        def teacher_step(i, total):
            at = span(i, TCH)
            value = jnp.exp2(nt(c_unit[at, :], weak_all[lanes, :]) * LOG2 - LOG2)
            teach[at, lanes] = value
            return total + fold(value)

        total = lax.fori_loop(0, classes // TCH, teacher_step, jnp.zeros((8, group_rows), F32), unroll=TUN)
        vec_t[0:1, lanes] = jnp.sum(total, axis=0, keepdims=True)
    to_blocks(vec_t[...], msg_a, 0)
    a_start(0)

    others = ints_all.at[pl.ds(0, nz - 1)]
    pltpu.make_async_copy(others, others, int_recv).wait()
    pltpu.make_async_copy(others, others, int_send).wait()
    offset = (z * ncls + cls) * classes
    for j in range(blocks):
        pair = ints_all[2 * j] + ints_all[2 * j + 1]
        label_row[0:1, j * LANES : (j + 1) * LANES] = pair[0:1, :] - offset
        flag_row[0:1, j * LANES : (j + 1) * LANES] = pair[1:2, :].astype(F32)

    for q in range(4):
        transpose_units(q)
    for away in range(2):
        pass_on(1, away)
    b_start(0)
    for away in range(2):
        sib_wait(1, away)

    def student_step(i, carry):
        total, label_dot = carry
        at = span(i, SCH)
        hit = hits(i, SCH)
        dot = nt(c_unit[at, :], strong_all[...])
        dot = jnp.where(hit, dot - MARGIN, dot)
        stud_dot[at, :] = dot
        value = jnp.exp2(dot * LOG2 - LOG2)
        stud_exp[at, :] = value
        return total + fold(value), label_dot + fold(jnp.where(hit, dot, 0.0))
    total, label_dot = lax.fori_loop(0, classes // SCH, student_step, (zero, zero), unroll=SUN)
    to_blocks(jnp.sum(total, axis=0, keepdims=True), msg_a, 1)
    a_start(1)
    to_blocks(SCALE * jnp.sum(label_dot, axis=0, keepdims=True), part_l, 0)
    to_row(1.0 / b_finish(0), vec_t)

    per_row = float(classes * nz * ncls) / rows

    def aligned_step(i, q_total):
        at = span(i)
        share = teach[at, :] * vec_t[...]
        batch = per_row * jnp.sum(share, axis=1, keepdims=True)
        fresh = MOMENTUM * marg_col[at, :] + (1.0 - MOMENTUM) * batch
        for j in range(CH // LANES):
            part = fresh[j * LANES : (j + 1) * LANES, :]
            fresh_out[pl.ds(i * (CH // LANES) + j, 1), :] = jnp.sum(jnp.where(eye, part, 0.0), axis=0, keepdims=True)
        inverse = 1.0 / fresh
        raw = share * jnp.concatenate([inverse] * blocks, axis=1)
        teach[at, :] = raw
        return q_total + fold(raw)
    q_total = lax.fori_loop(0, n_chunks, aligned_step, zero, unroll=2)
    to_blocks(jnp.sum(q_total, axis=0, keepdims=True), msg_a, 2)
    a_start(2)

    def cross_step(i, r_total):
        at = span(i)
        return r_total + fold(teach[at, :] * stud_dot[at, :])

    r_total = lax.fori_loop(0, n_chunks, cross_step, zero, unroll=2)
    to_blocks(SCALE * jnp.sum(r_total, axis=0, keepdims=True), part_r, 0)
    b_start(1)
    b_start(2)
    student_total = b_finish(1)
    to_row(1.0 / student_total, vec_e)
    vec_e[...] = vec_e[...] * flag_row[...]

    def share_step(i, carry):
        at = span(i)
        value = stud_exp[at, :] * vec_e[...]
        stud_exp[at, :] = jnp.where(hits(i), value - 0.5 * flag_row[...], value)
        return carry

    lax.fori_loop(0, n_chunks, share_step, 0, unroll=2)
    aligned_total = b_finish(2)
    to_row(-0.5 / aligned_total, vec_q)
    vec_q[...] = vec_q[...] * flag_row[...]

    flags_block = jnp.concatenate(
        [flag_row[0:1, j * LANES : (j + 1) * LANES] for j in range(blocks)], axis=0
    )
    loss_part = flags_block * (-0.5 * part_l[0] - 0.5 * part_r[0] / aligned_total)
    loss_tile = jnp.concatenate([loss_part, jnp.zeros((8 - blocks, LANES), F32)], axis=0)
    tile_rows = img // 8
    tile_cols = width // 2 // LANES
    per = tile_rows * tile_cols // nplane
    last = near * per

    def half_copy(part):
        return pltpu.make_async_remote_copy(
            half_buf.at[part, 1 - core], half_got.at[part], half_send.at[part], half_recv.at[part],
            device_id={"cls": sibling}, device_id_type=MESH,
        )

    def unit_half(part, which):
        at = pl.ds(pl.multiple_of(which * (width // 2), width // 2), width // 2)
        lanes = pl.ds(part * group_rows, group_rows)
        out = jnp.dot(c_unit_t[at, :], grad_t[:, lanes], preferred_element_type=F32).T
        for block in range(near):
            for t in range(tile_rows):
                for c in range(tile_cols):
                    index = t * tile_cols + c
                    row = block * img + t * 8
                    half_buf[part, which, index // per, block * per + index % per] = out[
                        row : row + 8, c * LANES : (c + 1) * LANES
                    ]
        for p in range(nplane):
            half_buf[part, which, p, last] = loss_tile

    def plane_start(part):
        half_copy(part).wait_recv()

        def half_add(p, carry):
            half_buf[part, core, p] = half_buf[part, core, p] + half_got[part, p]
            return carry

        lax.fori_loop(0, nplane, half_add, 0, unroll=True)

        def plane_copy(k, carry):
            p = lax.rem(plane + k, nplane)
            pltpu.make_async_remote_copy(
                half_buf.at[part, core, p], plane_got.at[part, plane], plane_send.at[part], plane_recv.at[part],
                device_id={"cls": p * 2 + core}, device_id_type=MESH,
            ).start()
            return carry

        lax.fori_loop(1, nplane, plane_copy, 0)
        plane_got[part, plane] = half_buf[part, core, plane]

    for part in range(2):
        lanes = pl.ds(part * group_rows, group_rows)

        def grad_step(i, carry):
            at = span(i)
            value = stud_exp[at, lanes] + teach[at, lanes] * vec_q[0:1, lanes]
            grad_t[at, lanes] = value.astype(BF16)
            return carry

        lax.fori_loop(0, n_chunks, grad_step, 0, unroll=2)
        if part == 1:
            plane_start(0)
        unit_half(part, 1 - core)
        half_copy(part).start()
        unit_half(part, core)
    plane_start(1)

    def center_step(i, carry):
        at = span(i)
        value = jnp.dot(grad_t[at, :], strong_all[...], preferred_element_type=F32)
        inverse = jnp.concatenate([c_inv[at, :]] * (width // LANES), axis=1)
        exact = c_raw[at, :].astype(F32) * inverse
        along = jnp.sum(exact * value, axis=1, keepdims=True)
        cgrad_out[at, :] = ((value - exact * along) * inverse).astype(BF16)
        return carry

    third = n_chunks * 5 // 8
    lax.fori_loop(0, third, center_step, 0, unroll=2)

    for part in range(2):
        whole = plane_got.at[part, pl.ds(0, nplane - 1)]
        pltpu.make_async_copy(whole, whole, plane_recv.at[part]).wait()
        plane_sum = jnp.sum(plane_got[part], axis=0)
        for block in range(near):
            z_send[part * near + block, 0:per] = plane_sum[block * per : (block + 1) * per]
    for block in range(nz):
        z_send[block, per] = plane_sum[last]
    z_got[z] = z_send[z]

    def z_copy(k, carry):
        to = lax.rem(z + k, nz)
        pltpu.make_async_remote_copy(
            z_send.at[to], z_got.at[z], z_send_sem, z_recv_sem, device_id={"dp": to}, device_id_type=MESH
        ).start()
        return carry

    lax.fori_loop(1, nz, z_copy, 0)

    two = n_chunks * 7 // 8
    lax.fori_loop(third, two, center_step, 0, unroll=2)

    whole_z = z_got.at[pl.ds(0, nz - 1)]
    pltpu.make_async_copy(whole_z, whole_z, z_recv_sem).wait()
    z_sum = jnp.sum(z_got[...], axis=0)
    tile_own[...] = z_sum[0:per]
    tile_got[cls] = z_sum[0:per]

    def tile_copy(k, carry):
        pltpu.make_async_remote_copy(
            tile_own, tile_got.at[cls], tile_send, tile_recv,
            device_id={"cls": lax.rem(cls + k, ncls)}, device_id_type=MESH,
        ).start()
        return carry

    lax.fori_loop(1, ncls, tile_copy, 0)
    lax.fori_loop(two, n_chunks, center_step, 0, unroll=2)
    loss_rows = flags_block * (SCALE + jnp.log(student_total)) + z_sum[per, 0:blocks, :]
    loss_out[...] = jnp.sum(jnp.sum(loss_rows, axis=1, keepdims=True), axis=0, keepdims=True) / img

    whole_t = tile_got.at[pl.ds(0, ncls - 1)]
    pltpu.make_async_copy(whole_t, whole_t, tile_recv).wait()
    bands = []
    for t in range(tile_rows):
        tiles = []
        for c in range(2 * tile_cols):
            index = t * tile_cols + c % tile_cols
            tiles.append(tile_got[(index // per) * 2 + c // tile_cols, index % per])
        bands.append(jnp.concatenate(tiles, axis=1))
    unit_grad = jnp.concatenate(bands, axis=0)
    exact, inverse = unit_rows(strong_own[...])
    egrad_out[...] = (unit_grad - exact * jnp.sum(exact * unit_grad, axis=1, keepdims=True)) * inverse
    for view in range(2):
        for away, k in sends:
            gather_copy(view, away, k).wait_send()
        for away in range(2):
            sent = sib_whole(view, away)
            pltpu.make_async_copy(sent, sent, sib_send.at[view, away]).wait()
    for n in range(3):
        sent = got_a.at[n, pl.ds(0, ncls - 1)]
        pltpu.make_async_copy(sent, sent, a_send.at[n]).wait()
        sent = got_b.at[n, pl.ds(0, nz - 1)]
        pltpu.make_async_copy(sent, sent, b_send.at[n]).wait()
    for part in range(2):
        half_copy(part).wait_send()
        sent = plane_got.at[part, pl.ds(0, nplane - 1)]
        pltpu.make_async_copy(sent, sent, plane_send.at[part]).wait()
    pltpu.make_async_copy(whole_z, whole_z, z_send_sem).wait()
    pltpu.make_async_copy(whole_t, whole_t, tile_send).wait()


def store(fresh_in, cgrad_in, egrad_in, loss_in, fresh_out, cgrad_out, egrad_out, loss_out, sem):
    parts = ((cgrad_in, cgrad_out), (egrad_in, egrad_out), (fresh_in, fresh_out), (loss_in, loss_out))
    copies = [pltpu.make_async_copy(a, b, sem.at[n]) for n, (a, b) in enumerate(parts)]
    for copy in copies:
        copy.start()
    for copy in copies:
        copy.wait()


def body(nz, ncls, weak_embed, strong_embed, centers, marginal, pseudo_label, confident):
    img, width = weak_embed.shape
    classes = centers.shape[0]
    rows = img * nz
    blocks = rows // LANES
    nplane = ncls // 2
    per = (img // 8) * (width // 2 // LANES) // nplane
    vmem = pltpu.VMEM
    dma = pltpu.SemaphoreType.DMA
    scratch = [
        vmem((img, width), BF16), vmem((img, width), BF16), vmem((2, img), jnp.int32), vmem((classes // LANES, LANES), F32),
        vmem((rows, width), BF16), vmem((rows, width), BF16), vmem((nz, 2, LANES), jnp.int32),
        vmem((1, rows), jnp.int32), vmem((1, rows), F32),
        vmem((classes, width), BF16), vmem((classes, width), BF16), vmem((width, classes), BF16),
        vmem((classes, LANES), F32), vmem((classes, LANES), F32),
        vmem((classes, rows), F32), vmem((classes, rows), F32), vmem((classes, rows), F32), vmem((classes, rows), BF16),
        vmem((1, rows), F32), vmem((1, rows), F32), vmem((1, rows), F32),
        vmem((3, blocks, LANES), F32), vmem((3, blocks, LANES), F32),
        vmem((3, ncls, blocks, LANES), F32), vmem((3, nz, blocks, LANES), F32),
        vmem((1, blocks, LANES), F32), vmem((1, blocks, LANES), F32),
        vmem((2, 2, nplane, nz // 2 * per + 1, 8, LANES), F32), vmem((2, nplane, nz // 2 * per + 1, 8, LANES), F32),
        vmem((2, nplane, nz // 2 * per + 1, 8, LANES), F32),
        vmem((nz, per + 1, 8, LANES), F32), vmem((nz, per + 1, 8, LANES), F32),
        vmem((per, 8, LANES), F32), vmem((ncls, per, 8, LANES), F32),
        dma((5,)), dma((4,)),
        dma((2, nz)), dma((2, nz)), dma((2, 2)), dma((2, 2)), dma, dma,
        dma((3,)), dma((3,)), dma((3,)), dma((3,)),
        dma((2,)), dma((2,)), dma((2,)), dma((2,)), dma, dma, dma, dma,
    ]
    hbm = pl.BlockSpec(memory_space=pl.ANY)
    local = pl.BlockSpec(memory_space=pltpu.VMEM)
    shapes = (((classes // LANES, LANES), F32), ((classes, width), BF16), ((img, width), F32), ((1, 1), F32))
    results = pl.pallas_call(
        functools.partial(kernel, nz, ncls),
        out_shape=tuple(pltpu.VMEM(*shape) for shape in shapes),
        in_specs=[hbm] * 6,
        out_specs=(local,) * 4,
        scratch_shapes=scratch,
        compiler_params=pltpu.CompilerParams(
            collective_id=0, has_side_effects=True, vmem_limit_bytes=55 * 1024 * 1024
        ),
    )(
        weak_embed, strong_embed, centers, marginal.reshape(classes // LANES, LANES),
        pseudo_label.reshape(1, img), confident.reshape(1, img),
    )
    fresh, cgrad, egrad, loss = pl.pallas_call(
        store,
        out_shape=tuple(jax.ShapeDtypeStruct(*shape) for shape in shapes),
        in_specs=[local] * 4,
        out_specs=(hbm,) * 4,
        scratch_shapes=[dma((4,))],
        compiler_params=pltpu.CompilerParams(vmem_limit_bytes=1024 * 1024),
    )(*results)
    return fresh.reshape(classes), cgrad, egrad, loss.reshape(())


def solution(mesh):
    placed = (
        P("dp", None),
        P("dp", None),
        P(("dp", "cls"), None),
        P(("dp", "cls")),
        P("dp"),
        P("dp"),
    )
    return jax.shard_map(
        functools.partial(body, mesh.shape["dp"], mesh.shape["cls"]),
        mesh=mesh,
        in_specs=placed,
        out_specs=(P(("dp", "cls")), P(("dp", "cls"), None), P("dp", None), P()),
        check_vma=False,
    )
```

```python
import functools
import math

import jax
import jax.numpy as jnp
from jax import lax
from jax.experimental import pallas as pl
from jax.experimental.pallas import tpu as pltpu
from jax.sharding import PartitionSpec as P

SCALE = 64.0
MARGIN = 0.35
MOMENTUM = 0.9
EPS = 1e-06
LOG2 = SCALE * math.log2(math.e)
MESH = pl.DeviceIdType.MESH
F32 = jnp.float32
BF16 = jnp.bfloat16
CH = 256
TCH, TUN = 256, 4
SCH, SUN = 256, 4
LANES = 128
PIECES = 2


def unit_rows(values):
    exact = values.astype(F32)
    inverse = lax.rsqrt(jnp.sum(exact * exact, axis=-1, keepdims=True) + EPS)
    return exact * inverse, inverse


def nt(a, b):
    return lax.dot_general(a, b, (((1,), (1,)), ((), ())), preferred_element_type=F32)


def kernel(
    nz, ncls,
    weak_hbm, strong_hbm, centers_hbm, marginal_hbm, label_hbm, flag_hbm,
    fresh_out, cgrad_out, egrad_out, loss_out,
    weak_own, strong_own, ints_own, marg,
    weak_all, strong_all, ints_all, label_row, flag_row,
    c_raw, c_unit, c_unit_t, c_inv, marg_col,
    teach, stud_dot, stud_exp, grad_t,
    vec_t, vec_q, vec_e,
    msg_a, msg_b, got_a, got_b,
    part_l, part_r, half_buf, half_got, plane_got, z_send, z_got, tile_own, tile_got,
    in_sem, c_sem,
    gather_send, gather_recv, sib_send, sib_recv, int_send, int_recv,
    a_send, a_recv, b_send, b_recv,
    half_send, half_recv, plane_send, plane_recv, z_send_sem, z_recv_sem, tile_send, tile_recv,
):
    img = weak_own.shape[0]
    half = img // 2
    classes = c_raw.shape[0]
    rows = weak_all.shape[0]
    width = weak_all.shape[1]
    blocks = rows // LANES
    nplane = ncls // 2
    z = lax.axis_index("dp")
    cls = lax.axis_index("cls")
    core = lax.rem(cls, 2)
    plane = lax.div(cls, 2)
    sibling = cls + 1 - 2 * core
    side = math.isqrt(nplane)
    x, y = lax.rem(plane, side), lax.div(plane, side)
    apart = [(dy, dx) for dy in range(side) for dx in range(nplane // side) if dy or dx]
    apart.sort(key=lambda d: -min(d[0], side - d[0]) - min(d[1], side - d[1]))
    planes = [lax.rem(y + dy, side) * side + lax.rem(x + dx, side) for dy, dx in apart]
    z_order = sorted(range(1, nz), key=lambda k: -min(k, nz - k))
    z_peers = [lax.rem(z + k, nz) for k in z_order]
    cls_peers = [p * 2 + c for p in planes for c in (core, 1 - core)] + [sibling]

    quarter = classes // 4
    own_copies = [
        pltpu.make_async_copy(weak_hbm, weak_own, in_sem.at[0]),
        pltpu.make_async_copy(strong_hbm, strong_own, in_sem.at[1]),
        pltpu.make_async_copy(label_hbm, ints_own.at[pl.ds(0, 1)], in_sem.at[2]),
        pltpu.make_async_copy(flag_hbm, ints_own.at[pl.ds(1, 1)], in_sem.at[3]),
        pltpu.make_async_copy(marginal_hbm, marg, in_sem.at[4]),
    ]
    for copy in own_copies:
        copy.start()
    c_copies = [
        pltpu.make_async_copy(
            centers_hbm.at[pl.ds(q * quarter, quarter)], c_raw.at[pl.ds(q * quarter, quarter)], c_sem.at[q]
        )
        for q in range(4)
    ]
    for copy in c_copies:
        copy.start()

    barrier = pltpu.get_barrier_semaphore()

    for peer in z_peers:
        pl.semaphore_signal(barrier, inc=1, device_id={"dp": peer}, device_id_type=MESH)
    for peer in cls_peers:
        pl.semaphore_signal(barrier, inc=1, device_id={"cls": peer}, device_id_type=MESH)

    base = pl.multiple_of(z * img, img)
    own_copies[0].wait()
    weak_exact, _ = unit_rows(weak_own[...])
    weak_all[pl.ds(base, img), :] = weak_exact.astype(BF16)
    pl.semaphore_wait(barrier, nz - 1 + ncls - 1)

    views = (weak_all, strong_all)
    near = nz // 2
    group, seat = lax.div(z, near), lax.rem(z, near)
    sends = [(away, k) for away in range(2) for k in range(near) if away or k]

    def piece(view, block):
        return views[view].at[pl.ds(pl.multiple_of(block * img + core * half, half), half)]

    def gather_copy(view, away, k):
        ref = piece(view, z)
        to = lax.rem(group + away, 2) * near + lax.rem(seat + k, near)
        at = away * near + k
        return pltpu.make_async_remote_copy(
            ref, ref, gather_send.at[view, at], gather_recv.at[view, at],
            device_id={"dp": to}, device_id_type=MESH,
        )

    def sib_copy(view, away, k):
        ref = piece(view, lax.rem(group + away, 2) * near + lax.rem(seat + near - k, near))
        return pltpu.make_async_remote_copy(
            ref, ref, sib_send.at[view, away], sib_recv.at[view, away],
            device_id={"cls": sibling}, device_id_type=MESH,
        )

    def int_copy(k, carry):
        pltpu.make_async_remote_copy(
            ints_all.at[z], ints_all.at[z], int_send, int_recv,
            device_id={"dp": lax.rem(z + k, nz)}, device_id_type=MESH,
        ).start()
        return carry

    for away, k in sends:
        gather_copy(0, away, k).start()
    own_copies[1].wait()
    strong_exact, _ = unit_rows(strong_own[...])
    strong_all[pl.ds(base, img), :] = strong_exact.astype(BF16)
    for away, k in sends:
        gather_copy(1, away, k).start()
    own_copies[2].wait()
    own_copies[3].wait()
    mine = ints_own[:, 0:img]
    both = jnp.concatenate([mine, mine], axis=1)
    lane = lax.broadcasted_iota(jnp.int32, both.shape, 1)
    ints_all[z] = jnp.where(lax.div(lane, img) == lax.rem(z, 2), both, 0)
    lax.fori_loop(1, nz, int_copy, 0)

    def pass_on(view, away):
        for k in range(near):
            if away or k:
                gather_copy(view, away, k).wait_recv()
                sib_copy(view, away, k).start()

    def sib_whole(view, away):
        return views[view].at[pl.ds(0, (near if away else near - 1) * half)]

    def sib_wait(view, away):
        whole = sib_whole(view, away)
        pltpu.make_async_copy(whole, whole, sib_recv.at[view, away]).wait()

    eye = lax.broadcasted_iota(jnp.int32, (LANES, LANES), 0) == lax.broadcasted_iota(jnp.int32, (LANES, LANES), 1)

    def prepare(q):
        c_copies[q].wait()

        def step(i, carry):
            at = pl.ds(pl.multiple_of(i * CH, CH), CH)
            exact, inv = unit_rows(c_raw[at, :])
            c_unit[at, :] = (exact * 1.0).astype(BF16)
            c_inv[at, :] = jnp.broadcast_to(inv, (CH, LANES))
            return carry

        lax.fori_loop(q * quarter // CH, (q + 1) * quarter // CH, step, 0)

    def transpose_units(q):
        def step(i, carry):
            at = pl.ds(pl.multiple_of(i * CH, CH), CH)
            c_unit_t[:, at] = c_unit[at, :].T
            return carry

        lax.fori_loop(q * quarter // CH, (q + 1) * quarter // CH, step, 0)

    def marginal_columns():
        own_copies[4].wait()

        def step(j, carry):
            row = jnp.broadcast_to(marg[pl.ds(j, 1), :], (LANES, LANES))
            column = jnp.sum(jnp.where(eye, row, 0.0), axis=1, keepdims=True)
            marg_col[pl.ds(pl.multiple_of(j * LANES, LANES), LANES), :] = jnp.broadcast_to(column, (LANES, LANES))
            return carry

        lax.fori_loop(0, classes // LANES, step, 0)

    for q in range(4):
        prepare(q)
    marginal_columns()

    def a_start(n):
        for peer in cls_peers:
            pltpu.make_async_remote_copy(
                msg_a.at[n], got_a.at[n, cls], a_send.at[n], a_recv.at[n],
                device_id={"cls": peer}, device_id_type=MESH,
            ).start()
        got_a[n, cls] = msg_a[n]

    def b_start(n):
        whole = got_a.at[n, pl.ds(0, ncls - 1)]
        pltpu.make_async_copy(whole, whole, a_recv.at[n]).wait()
        total = jnp.sum(got_a[n], axis=0)
        msg_b[n] = total
        for peer in z_peers:
            pltpu.make_async_remote_copy(
                msg_b.at[n], got_b.at[n, z], b_send.at[n], b_recv.at[n],
                device_id={"dp": peer}, device_id_type=MESH,
            ).start()
        got_b[n, z] = total

    def b_finish(n):
        whole = got_b.at[n, pl.ds(0, nz - 1)]
        pltpu.make_async_copy(whole, whole, b_recv.at[n]).wait()
        return jnp.sum(got_b[n], axis=0)

    def to_blocks(row, ref, n):
        for j in range(blocks):
            ref[n, j : j + 1, :] = row[:, j * LANES : (j + 1) * LANES]

    def to_row(block, ref):
        for j in range(blocks):
            ref[0:1, j * LANES : (j + 1) * LANES] = block[j : j + 1, :]

    def fold(value):
        return jnp.sum(value.reshape(value.shape[0] // 8, 8, value.shape[1]), axis=0)

    def span(i, size=CH):
        return pl.ds(pl.multiple_of(i * size, size), size)

    def hits(i, size=CH):
        ids = lax.broadcasted_iota(jnp.int32, (size, rows), 0) + i * size
        return ids == label_row[...]

    n_chunks = classes // CH
    zero = jnp.zeros((8, rows), F32)

    group_rows = rows // 2

    for away in range(2):
        pass_on(0, away)
        sib_wait(0, away)
        lanes = pl.ds(pl.multiple_of(lax.rem(group + away, 2) * group_rows, group_rows), group_rows)

        def teacher_step(i, total):
            at = span(i, TCH)
            value = jnp.exp2(nt(c_unit[at, :], weak_all[lanes, :]) * LOG2 - LOG2)
            teach[at, lanes] = value
            return total + fold(value)

        total = lax.fori_loop(0, classes // TCH, teacher_step, jnp.zeros((8, group_rows), F32), unroll=TUN)
        vec_t[0:1, lanes] = jnp.sum(total, axis=0, keepdims=True)
    to_blocks(vec_t[...], msg_a, 0)
    a_start(0)

    others = ints_all.at[pl.ds(0, nz - 1)]
    pltpu.make_async_copy(others, others, int_recv).wait()
    pltpu.make_async_copy(others, others, int_send).wait()
    offset = (z * ncls + cls) * classes
    for j in range(blocks):
        pair = ints_all[2 * j] + ints_all[2 * j + 1]
        label_row[0:1, j * LANES : (j + 1) * LANES] = pair[0:1, :] - offset
        flag_row[0:1, j * LANES : (j + 1) * LANES] = pair[1:2, :].astype(F32)

    for q in range(4):
        transpose_units(q)
    for away in range(2):
        pass_on(1, away)
    b_start(0)
    for away in range(2):
        sib_wait(1, away)

    def student_step(i, carry):
        total, label_dot = carry
        at = span(i, SCH)
        hit = hits(i, SCH)
        dot = nt(c_unit[at, :], strong_all[...])
        dot = jnp.where(hit, dot - MARGIN, dot)
        stud_dot[at, :] = dot
        value = jnp.exp2(dot * LOG2 - LOG2)
        stud_exp[at, :] = value
        return total + fold(value), label_dot + fold(jnp.where(hit, dot, 0.0))
    total, label_dot = lax.fori_loop(0, classes // SCH, student_step, (zero, zero), unroll=SUN)
    to_blocks(jnp.sum(total, axis=0, keepdims=True), msg_a, 1)
    a_start(1)
    to_blocks(SCALE * jnp.sum(label_dot, axis=0, keepdims=True), part_l, 0)
    to_row(1.0 / b_finish(0), vec_t)

    per_row = float(classes * nz * ncls) / rows

    def aligned_step(i, q_total):
        at = span(i)
        share = teach[at, :] * vec_t[...]
        batch = per_row * jnp.sum(share, axis=1, keepdims=True)
        fresh = MOMENTUM * marg_col[at, :] + (1.0 - MOMENTUM) * batch
        for j in range(CH // LANES):
            part = fresh[j * LANES : (j + 1) * LANES, :]
            fresh_out[pl.ds(i * (CH // LANES) + j, 1), :] = jnp.sum(jnp.where(eye, part, 0.0), axis=0, keepdims=True)
        inverse = 1.0 / fresh
        raw = share * jnp.concatenate([inverse] * blocks, axis=1)
        teach[at, :] = raw
        return q_total + fold(raw)
    q_total = lax.fori_loop(0, n_chunks, aligned_step, zero, unroll=2)
    to_blocks(jnp.sum(q_total, axis=0, keepdims=True), msg_a, 2)
    a_start(2)

    def cross_step(i, r_total):
        at = span(i)
        return r_total + fold(teach[at, :] * stud_dot[at, :])

    r_total = lax.fori_loop(0, n_chunks, cross_step, zero, unroll=2)
    to_blocks(SCALE * jnp.sum(r_total, axis=0, keepdims=True), part_r, 0)
    b_start(1)
    b_start(2)
    student_total = b_finish(1)
    to_row(1.0 / student_total, vec_e)
    vec_e[...] = vec_e[...] * flag_row[...]

    def share_step(i, carry):
        at = span(i)
        value = stud_exp[at, :] * vec_e[...]
        stud_exp[at, :] = jnp.where(hits(i), value - 0.5 * flag_row[...], value)
        return carry

    lax.fori_loop(0, n_chunks, share_step, 0, unroll=2)
    aligned_total = b_finish(2)
    to_row(-0.5 / aligned_total, vec_q)
    vec_q[...] = vec_q[...] * flag_row[...]

    flags_block = jnp.concatenate(
        [flag_row[0:1, j * LANES : (j + 1) * LANES] for j in range(blocks)], axis=0
    )
    loss_part = flags_block * (-0.5 * part_l[0] - 0.5 * part_r[0] / aligned_total)
    loss_tile = jnp.concatenate([loss_part, jnp.zeros((8 - blocks, LANES), F32)], axis=0)
    tile_rows = img // 8
    tile_cols = width // 2 // LANES
    per = tile_rows * tile_cols // nplane
    last = near * per

    def half_copy(part):
        return pltpu.make_async_remote_copy(
            half_buf.at[part, 1 - core], half_got.at[part], half_send.at[part], half_recv.at[part],
            device_id={"cls": sibling}, device_id_type=MESH,
        )

    def unit_half(part, which):
        at = pl.ds(pl.multiple_of(which * (width // 2), width // 2), width // 2)
        lanes = pl.ds(part * group_rows, group_rows)
        out = jnp.dot(c_unit_t[at, :], grad_t[:, lanes], preferred_element_type=F32).T
        for block in range(near):
            for t in range(tile_rows):
                for c in range(tile_cols):
                    index = t * tile_cols + c
                    row = block * img + t * 8
                    half_buf[part, which, index // per, block * per + index % per] = out[
                        row : row + 8, c * LANES : (c + 1) * LANES
                    ]
        for p in range(nplane):
            half_buf[part, which, p, last] = loss_tile

    def plane_start(part):
        half_copy(part).wait_recv()

        def half_add(p, carry):
            half_buf[part, core, p] = half_buf[part, core, p] + half_got[part, p]
            return carry

        lax.fori_loop(0, nplane, half_add, 0, unroll=True)

        for p in planes:
            pltpu.make_async_remote_copy(
                half_buf.at[part, core, p], plane_got.at[part, plane], plane_send.at[part], plane_recv.at[part],
                device_id={"cls": p * 2 + core}, device_id_type=MESH,
            ).start()
        plane_got[part, plane] = half_buf[part, core, plane]

    for part in range(2):
        lanes = pl.ds(part * group_rows, group_rows)

        def grad_step(i, carry):
            at = span(i)
            value = stud_exp[at, lanes] + teach[at, lanes] * vec_q[0:1, lanes]
            grad_t[at, lanes] = value.astype(BF16)
            return carry

        lax.fori_loop(0, n_chunks, grad_step, 0, unroll=2)
        if part == 1:
            plane_start(0)
        unit_half(part, 1 - core)
        half_copy(part).start()
        unit_half(part, core)
    plane_start(1)

    def center_step(i, carry):
        at = span(i)
        value = jnp.dot(grad_t[at, :], strong_all[...], preferred_element_type=F32)
        inverse = jnp.concatenate([c_inv[at, :]] * (width // LANES), axis=1)
        exact = c_raw[at, :].astype(F32) * inverse
        along = jnp.sum(exact * value, axis=1, keepdims=True)
        cgrad_out[at, :] = ((value - exact * along) * inverse).astype(BF16)
        return carry

    third = n_chunks * 5 // 8
    lax.fori_loop(0, third, center_step, 0, unroll=2)

    for part in range(2):
        whole = plane_got.at[part, pl.ds(0, nplane - 1)]
        pltpu.make_async_copy(whole, whole, plane_recv.at[part]).wait()
        plane_sum = jnp.sum(plane_got[part], axis=0)
        for block in range(near):
            z_send[part * near + block, 0:per] = plane_sum[block * per : (block + 1) * per]
    for block in range(nz):
        z_send[block, per] = plane_sum[last]
    for to in z_peers:
        pltpu.make_async_remote_copy(
            z_send.at[to], z_got.at[z], z_send_sem, z_recv_sem, device_id={"dp": to}, device_id_type=MESH
        ).start()
    z_got[z] = z_send[z]

    two = n_chunks * 7 // 8
    lax.fori_loop(third, two, center_step, 0, unroll=2)

    whole_z = z_got.at[pl.ds(0, nz - 1)]
    pltpu.make_async_copy(whole_z, whole_z, z_recv_sem).wait()
    z_sum = jnp.sum(z_got[...], axis=0)
    tile_own[...] = z_sum[0:per]
    for peer in cls_peers:
        pltpu.make_async_remote_copy(
            tile_own, tile_got.at[cls], tile_send, tile_recv, device_id={"cls": peer}, device_id_type=MESH
        ).start()
    tile_got[cls] = z_sum[0:per]

    lax.fori_loop(two, n_chunks, center_step, 0, unroll=2)
    loss_rows = flags_block * (SCALE + jnp.log(student_total)) + z_sum[per, 0:blocks, :]
    loss_out[...] = jnp.sum(jnp.sum(loss_rows, axis=1, keepdims=True), axis=0, keepdims=True) / img

    whole_t = tile_got.at[pl.ds(0, ncls - 1)]
    pltpu.make_async_copy(whole_t, whole_t, tile_recv).wait()
    bands = []
    for t in range(tile_rows):
        tiles = []
        for c in range(2 * tile_cols):
            index = t * tile_cols + c % tile_cols
            tiles.append(tile_got[(index // per) * 2 + c // tile_cols, index % per])
        bands.append(jnp.concatenate(tiles, axis=1))
    unit_grad = jnp.concatenate(bands, axis=0)
    exact, inverse = unit_rows(strong_own[...])
    egrad_out[...] = (unit_grad - exact * jnp.sum(exact * unit_grad, axis=1, keepdims=True)) * inverse
    for view in range(2):
        for away, k in sends:
            gather_copy(view, away, k).wait_send()
        for away in range(2):
            sent = sib_whole(view, away)
            pltpu.make_async_copy(sent, sent, sib_send.at[view, away]).wait()
    for n in range(3):
        sent = got_a.at[n, pl.ds(0, ncls - 1)]
        pltpu.make_async_copy(sent, sent, a_send.at[n]).wait()
        sent = got_b.at[n, pl.ds(0, nz - 1)]
        pltpu.make_async_copy(sent, sent, b_send.at[n]).wait()
    for part in range(2):
        half_copy(part).wait_send()
        sent = plane_got.at[part, pl.ds(0, nplane - 1)]
        pltpu.make_async_copy(sent, sent, plane_send.at[part]).wait()
    pltpu.make_async_copy(whole_z, whole_z, z_send_sem).wait()
    pltpu.make_async_copy(whole_t, whole_t, tile_send).wait()


def store(fresh_in, cgrad_in, egrad_in, loss_in, fresh_out, cgrad_out, egrad_out, loss_out, sem):
    size = cgrad_in.shape[0] // PIECES
    parts = [(cgrad_in.at[pl.ds(n * size, size)], cgrad_out.at[pl.ds(n * size, size)]) for n in range(PIECES)]
    parts += [(egrad_in, egrad_out), (fresh_in, fresh_out), (loss_in, loss_out)]
    copies = [pltpu.make_async_copy(a, b, sem.at[n]) for n, (a, b) in enumerate(parts)]
    for copy in copies:
        copy.start()
    for copy in copies:
        copy.wait()


def body(nz, ncls, weak_embed, strong_embed, centers, marginal, pseudo_label, confident):
    img, width = weak_embed.shape
    classes = centers.shape[0]
    rows = img * nz
    blocks = rows // LANES
    nplane = ncls // 2
    per = (img // 8) * (width // 2 // LANES) // nplane
    vmem = pltpu.VMEM
    dma = pltpu.SemaphoreType.DMA
    scratch = [
        vmem((img, width), BF16), vmem((img, width), BF16), vmem((2, img), jnp.int32), vmem((classes // LANES, LANES), F32),
        vmem((rows, width), BF16), vmem((rows, width), BF16), vmem((nz, 2, LANES), jnp.int32),
        vmem((1, rows), jnp.int32), vmem((1, rows), F32),
        vmem((classes, width), BF16), vmem((classes, width), BF16), vmem((width, classes), BF16),
        vmem((classes, LANES), F32), vmem((classes, LANES), F32),
        vmem((classes, rows), F32), vmem((classes, rows), F32), vmem((classes, rows), F32), vmem((classes, rows), BF16),
        vmem((1, rows), F32), vmem((1, rows), F32), vmem((1, rows), F32),
        vmem((3, blocks, LANES), F32), vmem((3, blocks, LANES), F32),
        vmem((3, ncls, blocks, LANES), F32), vmem((3, nz, blocks, LANES), F32),
        vmem((1, blocks, LANES), F32), vmem((1, blocks, LANES), F32),
        vmem((2, 2, nplane, nz // 2 * per + 1, 8, LANES), F32), vmem((2, nplane, nz // 2 * per + 1, 8, LANES), F32),
        vmem((2, nplane, nz // 2 * per + 1, 8, LANES), F32),
        vmem((nz, per + 1, 8, LANES), F32), vmem((nz, per + 1, 8, LANES), F32),
        vmem((per, 8, LANES), F32), vmem((ncls, per, 8, LANES), F32),
        dma((5,)), dma((4,)),
        dma((2, nz)), dma((2, nz)), dma((2, 2)), dma((2, 2)), dma, dma,
        dma((3,)), dma((3,)), dma((3,)), dma((3,)),
        dma((2,)), dma((2,)), dma((2,)), dma((2,)), dma, dma, dma, dma,
    ]
    hbm = pl.BlockSpec(memory_space=pl.ANY)
    local = pl.BlockSpec(memory_space=pltpu.VMEM)
    shapes = (((classes // LANES, LANES), F32), ((classes, width), BF16), ((img, width), F32), ((1, 1), F32))
    results = pl.pallas_call(
        functools.partial(kernel, nz, ncls),
        out_shape=tuple(pltpu.VMEM(*shape) for shape in shapes),
        in_specs=[hbm] * 6,
        out_specs=(local,) * 4,
        scratch_shapes=scratch,
        compiler_params=pltpu.CompilerParams(
            collective_id=0, has_side_effects=True, vmem_limit_bytes=55 * 1024 * 1024
        ),
    )(
        weak_embed, strong_embed, centers, marginal.reshape(classes // LANES, LANES),
        pseudo_label.reshape(1, img), confident.reshape(1, img),
    )
    fresh, cgrad, egrad, loss = pl.pallas_call(
        store,
        out_shape=tuple(jax.ShapeDtypeStruct(*shape) for shape in shapes),
        in_specs=[local] * 4,
        out_specs=(hbm,) * 4,
        scratch_shapes=[dma((PIECES + 3,))],
        compiler_params=pltpu.CompilerParams(vmem_limit_bytes=1024 * 1024),
    )(*results)
    return fresh.reshape(classes), cgrad, egrad, loss.reshape(())


def solution(mesh):
    placed = (
        P("dp", None),
        P("dp", None),
        P(("dp", "cls"), None),
        P(("dp", "cls")),
        P("dp"),
        P("dp"),
    )
    return jax.shard_map(
        functools.partial(body, mesh.shape["dp"], mesh.shape["cls"]),
        mesh=mesh,
        in_specs=placed,
        out_specs=(P(("dp", "cls")), P(("dp", "cls"), None), P("dp", None), P()),
        check_vma=False,
    )
```

```python
import functools
import math

import jax
import jax.numpy as jnp
from jax import lax
from jax.experimental import pallas as pl
from jax.experimental.pallas import tpu as pltpu
from jax.sharding import PartitionSpec as P

SCALE = 64.0
MARGIN = 0.35
MOMENTUM = 0.9
EPS = 1e-06
LOG2 = SCALE * math.log2(math.e)
MESH = pl.DeviceIdType.MESH
F32 = jnp.float32
BF16 = jnp.bfloat16
CH = 256
TCH, TUN = 256, 4
SCH, SUN = 256, 4
LANES = 128
PIECES = 2


def unit_rows(values):
    exact = values.astype(F32)
    inverse = lax.rsqrt(jnp.sum(exact * exact, axis=-1, keepdims=True) + EPS)
    return exact * inverse, inverse


def nt(a, b):
    return lax.dot_general(a, b, (((1,), (1,)), ((), ())), preferred_element_type=F32)


def kernel(
    nz, ncls,
    weak_hbm, strong_hbm, centers_hbm, marginal_hbm, label_hbm, flag_hbm,
    fresh_out, cgrad_out, egrad_out, loss_out,
    weak_own, strong_own, ints_own, marg,
    weak_all, strong_all, ints_all, label_row, flag_row,
    c_raw, c_unit, c_unit_t, c_inv, marg_col,
    teach, stud_dot, stud_exp, grad_t,
    vec_t, vec_q, vec_e,
    msg_a, msg_b, got_a, got_b,
    part_l, part_r, half_buf, half_got, plane_got, z_send, z_got, tile_own, tile_got,
    in_sem, c_sem,
    gather_send, gather_recv, sib_send, sib_recv, int_send, int_recv,
    a_send, a_recv, b_send, b_recv,
    half_send, half_recv, plane_send, plane_recv, z_send_sem, z_recv_sem, tile_send, tile_recv,
):
    img = weak_own.shape[0]
    half = img // 2
    classes = c_raw.shape[0]
    rows = weak_all.shape[0]
    width = weak_all.shape[1]
    blocks = rows // LANES
    nplane = ncls // 2
    z = lax.axis_index("dp")
    cls = lax.axis_index("cls")
    core = lax.rem(cls, 2)
    plane = lax.div(cls, 2)
    sibling = cls + 1 - 2 * core
    side = math.isqrt(nplane)
    x, y = lax.rem(plane, side), lax.div(plane, side)
    apart = [(dy, dx) for dy in range(side) for dx in range(nplane // side) if dy or dx]
    apart.sort(key=lambda d: -min(d[0], side - d[0]) - min(d[1], side - d[1]))
    planes = [lax.rem(y + dy, side) * side + lax.rem(x + dx, side) for dy, dx in apart]
    z_order = sorted(range(1, nz), key=lambda k: -min(k, nz - k))
    z_peers = [lax.rem(z + k, nz) for k in z_order]
    cls_peers = [p * 2 + c for p in planes for c in (core, 1 - core)] + [sibling]

    quarter = classes // 4
    own_copies = [
        pltpu.make_async_copy(weak_hbm, weak_own, in_sem.at[0]),
        pltpu.make_async_copy(strong_hbm, strong_own, in_sem.at[1]),
        pltpu.make_async_copy(label_hbm, ints_own.at[pl.ds(0, 1)], in_sem.at[2]),
        pltpu.make_async_copy(flag_hbm, ints_own.at[pl.ds(1, 1)], in_sem.at[3]),
        pltpu.make_async_copy(marginal_hbm, marg, in_sem.at[4]),
    ]
    for copy in own_copies:
        copy.start()
    c_copies = [
        pltpu.make_async_copy(
            centers_hbm.at[pl.ds(q * quarter, quarter)], c_raw.at[pl.ds(q * quarter, quarter)], c_sem.at[q]
        )
        for q in range(4)
    ]
    for copy in c_copies:
        copy.start()

    barrier = pltpu.get_barrier_semaphore()

    for peer in z_peers:
        pl.semaphore_signal(barrier, inc=1, device_id={"dp": peer}, device_id_type=MESH)
    for peer in cls_peers:
        pl.semaphore_signal(barrier, inc=1, device_id={"cls": peer}, device_id_type=MESH)

    base = pl.multiple_of(z * img, img)
    own_copies[0].wait()
    weak_exact, _ = unit_rows(weak_own[...])
    weak_all[pl.ds(base, img), :] = weak_exact.astype(BF16)
    pl.semaphore_wait(barrier, nz - 1 + ncls - 1)

    views = (weak_all, strong_all)
    near = nz // 2
    group, seat = lax.div(z, near), lax.rem(z, near)
    sends = [(away, k) for away in range(2) for k in range(near) if away or k]

    def piece(view, block):
        return views[view].at[pl.ds(pl.multiple_of(block * img + core * half, half), half)]

    def gather_copy(view, away, k):
        ref = piece(view, z)
        to = lax.rem(group + away, 2) * near + lax.rem(seat + k, near)
        at = away * near + k
        return pltpu.make_async_remote_copy(
            ref, ref, gather_send.at[view, at], gather_recv.at[view, at],
            device_id={"dp": to}, device_id_type=MESH,
        )

    def sib_copy(view, away, k):
        ref = piece(view, lax.rem(group + away, 2) * near + lax.rem(seat + near - k, near))
        return pltpu.make_async_remote_copy(
            ref, ref, sib_send.at[view, away], sib_recv.at[view, away],
            device_id={"cls": sibling}, device_id_type=MESH,
        )

    def int_copy(k, carry):
        pltpu.make_async_remote_copy(
            ints_all.at[z], ints_all.at[z], int_send, int_recv,
            device_id={"dp": lax.rem(z + k, nz)}, device_id_type=MESH,
        ).start()
        return carry

    for away, k in sends:
        gather_copy(0, away, k).start()
    own_copies[1].wait()
    strong_exact, _ = unit_rows(strong_own[...])
    strong_all[pl.ds(base, img), :] = strong_exact.astype(BF16)
    own_copies[2].wait()
    own_copies[3].wait()
    mine = ints_own[:, 0:img]
    both = jnp.concatenate([mine, mine], axis=1)
    lane = lax.broadcasted_iota(jnp.int32, both.shape, 1)
    ints_all[z] = jnp.where(lax.div(lane, img) == lax.rem(z, 2), both, 0)
    lax.fori_loop(1, nz, int_copy, 0)

    def pass_on(view, away):
        for k in range(near):
            if away or k:
                gather_copy(view, away, k).wait_recv()
                sib_copy(view, away, k).start()

    def sib_whole(view, away):
        return views[view].at[pl.ds(0, (near if away else near - 1) * half)]

    def sib_wait(view, away):
        whole = sib_whole(view, away)
        pltpu.make_async_copy(whole, whole, sib_recv.at[view, away]).wait()

    eye = lax.broadcasted_iota(jnp.int32, (LANES, LANES), 0) == lax.broadcasted_iota(jnp.int32, (LANES, LANES), 1)

    def prepare(q):
        c_copies[q].wait()

        def step(i, carry):
            at = pl.ds(pl.multiple_of(i * CH, CH), CH)
            exact, inv = unit_rows(c_raw[at, :])
            c_unit[at, :] = (exact * 1.0).astype(BF16)
            c_inv[at, :] = jnp.broadcast_to(inv, (CH, LANES))
            return carry

        lax.fori_loop(q * quarter // CH, (q + 1) * quarter // CH, step, 0)

    def transpose_units(q):
        def step(i, carry):
            at = pl.ds(pl.multiple_of(i * CH, CH), CH)
            c_unit_t[:, at] = c_unit[at, :].T
            return carry

        lax.fori_loop(q * quarter // CH, (q + 1) * quarter // CH, step, 0)

    def marginal_columns():
        own_copies[4].wait()

        def step(j, carry):
            row = jnp.broadcast_to(marg[pl.ds(j, 1), :], (LANES, LANES))
            column = jnp.sum(jnp.where(eye, row, 0.0), axis=1, keepdims=True)
            marg_col[pl.ds(pl.multiple_of(j * LANES, LANES), LANES), :] = jnp.broadcast_to(column, (LANES, LANES))
            return carry

        lax.fori_loop(0, classes // LANES, step, 0)

    for q in range(4):
        prepare(q)
    marginal_columns()

    def a_start(n):
        for peer in cls_peers:
            pltpu.make_async_remote_copy(
                msg_a.at[n], got_a.at[n, cls], a_send.at[n], a_recv.at[n],
                device_id={"cls": peer}, device_id_type=MESH,
            ).start()
        got_a[n, cls] = msg_a[n]

    def b_start(n):
        whole = got_a.at[n, pl.ds(0, ncls - 1)]
        pltpu.make_async_copy(whole, whole, a_recv.at[n]).wait()
        total = jnp.sum(got_a[n], axis=0)
        msg_b[n] = total
        for peer in z_peers:
            pltpu.make_async_remote_copy(
                msg_b.at[n], got_b.at[n, z], b_send.at[n], b_recv.at[n],
                device_id={"dp": peer}, device_id_type=MESH,
            ).start()
        got_b[n, z] = total

    def b_finish(n):
        whole = got_b.at[n, pl.ds(0, nz - 1)]
        pltpu.make_async_copy(whole, whole, b_recv.at[n]).wait()
        return jnp.sum(got_b[n], axis=0)

    def to_blocks(row, ref, n):
        for j in range(blocks):
            ref[n, j : j + 1, :] = row[:, j * LANES : (j + 1) * LANES]

    def to_row(block, ref):
        for j in range(blocks):
            ref[0:1, j * LANES : (j + 1) * LANES] = block[j : j + 1, :]

    def fold(value):
        return jnp.sum(value.reshape(value.shape[0] // 8, 8, value.shape[1]), axis=0)

    def span(i, size=CH):
        return pl.ds(pl.multiple_of(i * size, size), size)

    def hits(i, size=CH):
        ids = lax.broadcasted_iota(jnp.int32, (size, rows), 0) + i * size
        return ids == label_row[...]

    n_chunks = classes // CH
    zero = jnp.zeros((8, rows), F32)

    for away, k in sends:
        gather_copy(1, away, k).start()

    group_rows = rows // 2

    for away in range(2):
        pass_on(0, away)
        sib_wait(0, away)
        lanes = pl.ds(pl.multiple_of(lax.rem(group + away, 2) * group_rows, group_rows), group_rows)

        def teacher_step(i, total):
            at = span(i, TCH)
            value = jnp.exp2(nt(c_unit[at, :], weak_all[lanes, :]) * LOG2 - LOG2)
            teach[at, lanes] = value
            return total + fold(value)

        total = lax.fori_loop(0, classes // TCH, teacher_step, jnp.zeros((8, group_rows), F32), unroll=TUN)
        vec_t[0:1, lanes] = jnp.sum(total, axis=0, keepdims=True)
    to_blocks(vec_t[...], msg_a, 0)
    a_start(0)

    others = ints_all.at[pl.ds(0, nz - 1)]
    pltpu.make_async_copy(others, others, int_recv).wait()
    pltpu.make_async_copy(others, others, int_send).wait()
    offset = (z * ncls + cls) * classes
    for j in range(blocks):
        pair = ints_all[2 * j] + ints_all[2 * j + 1]
        label_row[0:1, j * LANES : (j + 1) * LANES] = pair[0:1, :] - offset
        flag_row[0:1, j * LANES : (j + 1) * LANES] = pair[1:2, :].astype(F32)

    for q in range(4):
        transpose_units(q)
    for away in range(2):
        pass_on(1, away)
    b_start(0)
    for away in range(2):
        sib_wait(1, away)

    def student_step(i, carry):
        total, label_dot = carry
        at = span(i, SCH)
        hit = hits(i, SCH)
        dot = nt(c_unit[at, :], strong_all[...])
        dot = jnp.where(hit, dot - MARGIN, dot)
        stud_dot[at, :] = dot
        value = jnp.exp2(dot * LOG2 - LOG2)
        stud_exp[at, :] = value
        return total + fold(value), label_dot + fold(jnp.where(hit, dot, 0.0))
    total, label_dot = lax.fori_loop(0, classes // SCH, student_step, (zero, zero), unroll=SUN)
    to_blocks(jnp.sum(total, axis=0, keepdims=True), msg_a, 1)
    a_start(1)
    to_blocks(SCALE * jnp.sum(label_dot, axis=0, keepdims=True), part_l, 0)
    to_row(1.0 / b_finish(0), vec_t)

    per_row = float(classes * nz * ncls) / rows

    def aligned_step(i, q_total):
        at = span(i)
        share = teach[at, :] * vec_t[...]
        batch = per_row * jnp.sum(share, axis=1, keepdims=True)
        fresh = MOMENTUM * marg_col[at, :] + (1.0 - MOMENTUM) * batch
        for j in range(CH // LANES):
            part = fresh[j * LANES : (j + 1) * LANES, :]
            fresh_out[pl.ds(i * (CH // LANES) + j, 1), :] = jnp.sum(jnp.where(eye, part, 0.0), axis=0, keepdims=True)
        inverse = 1.0 / fresh
        raw = share * jnp.concatenate([inverse] * blocks, axis=1)
        teach[at, :] = raw
        return q_total + fold(raw)
    q_total = lax.fori_loop(0, n_chunks, aligned_step, zero, unroll=2)
    to_blocks(jnp.sum(q_total, axis=0, keepdims=True), msg_a, 2)
    a_start(2)

    def cross_step(i, r_total):
        at = span(i)
        return r_total + fold(teach[at, :] * stud_dot[at, :])

    r_total = lax.fori_loop(0, n_chunks, cross_step, zero, unroll=2)
    to_blocks(SCALE * jnp.sum(r_total, axis=0, keepdims=True), part_r, 0)
    b_start(1)
    b_start(2)
    student_total = b_finish(1)
    to_row(1.0 / student_total, vec_e)
    vec_e[...] = vec_e[...] * flag_row[...]

    def share_step(i, carry):
        at = span(i)
        value = stud_exp[at, :] * vec_e[...]
        stud_exp[at, :] = jnp.where(hits(i), value - 0.5 * flag_row[...], value)
        return carry

    lax.fori_loop(0, n_chunks, share_step, 0, unroll=2)
    aligned_total = b_finish(2)
    to_row(-0.5 / aligned_total, vec_q)
    vec_q[...] = vec_q[...] * flag_row[...]

    flags_block = jnp.concatenate(
        [flag_row[0:1, j * LANES : (j + 1) * LANES] for j in range(blocks)], axis=0
    )
    loss_part = flags_block * (-0.5 * part_l[0] - 0.5 * part_r[0] / aligned_total)
    loss_tile = jnp.concatenate([loss_part, jnp.zeros((8 - blocks, LANES), F32)], axis=0)
    tile_rows = img // 8
    tile_cols = width // 2 // LANES
    per = tile_rows * tile_cols // nplane
    last = near * per

    def half_copy(part):
        return pltpu.make_async_remote_copy(
            half_buf.at[part, 1 - core], half_got.at[part], half_send.at[part], half_recv.at[part],
            device_id={"cls": sibling}, device_id_type=MESH,
        )

    def unit_half(part, which):
        at = pl.ds(pl.multiple_of(which * (width // 2), width // 2), width // 2)
        lanes = pl.ds(part * group_rows, group_rows)
        out = jnp.dot(c_unit_t[at, :], grad_t[:, lanes], preferred_element_type=F32).T
        for block in range(near):
            for t in range(tile_rows):
                for c in range(tile_cols):
                    index = t * tile_cols + c
                    row = block * img + t * 8
                    half_buf[part, which, index // per, block * per + index % per] = out[
                        row : row + 8, c * LANES : (c + 1) * LANES
                    ]
        for p in range(nplane):
            half_buf[part, which, p, last] = loss_tile

    def plane_start(part):
        half_copy(part).wait_recv()

        def half_add(p, carry):
            half_buf[part, core, p] = half_buf[part, core, p] + half_got[part, p]
            return carry

        lax.fori_loop(0, nplane, half_add, 0, unroll=True)

        for p in planes:
            pltpu.make_async_remote_copy(
                half_buf.at[part, core, p], plane_got.at[part, plane], plane_send.at[part], plane_recv.at[part],
                device_id={"cls": p * 2 + core}, device_id_type=MESH,
            ).start()
        plane_got[part, plane] = half_buf[part, core, plane]

    for part in range(2):
        lanes = pl.ds(part * group_rows, group_rows)

        def grad_step(i, carry):
            at = span(i)
            value = stud_exp[at, lanes] + teach[at, lanes] * vec_q[0:1, lanes]
            grad_t[at, lanes] = value.astype(BF16)
            return carry

        lax.fori_loop(0, n_chunks, grad_step, 0, unroll=2)
        if part == 1:
            plane_start(0)
        unit_half(part, 1 - core)
        half_copy(part).start()
        unit_half(part, core)
    plane_start(1)

    def center_step(i, carry):
        at = span(i)
        value = jnp.dot(grad_t[at, :], strong_all[...], preferred_element_type=F32)
        inverse = jnp.concatenate([c_inv[at, :]] * (width // LANES), axis=1)
        exact = c_raw[at, :].astype(F32) * inverse
        along = jnp.sum(exact * value, axis=1, keepdims=True)
        cgrad_out[at, :] = ((value - exact * along) * inverse).astype(BF16)
        return carry

    third = n_chunks * 5 // 8
    lax.fori_loop(0, third, center_step, 0, unroll=2)

    for part in range(2):
        whole = plane_got.at[part, pl.ds(0, nplane - 1)]
        pltpu.make_async_copy(whole, whole, plane_recv.at[part]).wait()
        plane_sum = jnp.sum(plane_got[part], axis=0)
        for block in range(near):
            z_send[part * near + block, 0:per] = plane_sum[block * per : (block + 1) * per]
    for block in range(nz):
        z_send[block, per] = plane_sum[last]
    for to in z_peers:
        pltpu.make_async_remote_copy(
            z_send.at[to], z_got.at[z], z_send_sem, z_recv_sem, device_id={"dp": to}, device_id_type=MESH
        ).start()
    z_got[z] = z_send[z]

    two = n_chunks * 7 // 8
    lax.fori_loop(third, two, center_step, 0, unroll=2)

    whole_z = z_got.at[pl.ds(0, nz - 1)]
    pltpu.make_async_copy(whole_z, whole_z, z_recv_sem).wait()
    z_sum = jnp.sum(z_got[...], axis=0)
    tile_own[...] = z_sum[0:per]
    for peer in cls_peers:
        pltpu.make_async_remote_copy(
            tile_own, tile_got.at[cls], tile_send, tile_recv, device_id={"cls": peer}, device_id_type=MESH
        ).start()
    tile_got[cls] = z_sum[0:per]

    lax.fori_loop(two, n_chunks, center_step, 0, unroll=2)
    loss_rows = flags_block * (SCALE + jnp.log(student_total)) + z_sum[per, 0:blocks, :]
    loss_out[...] = jnp.sum(jnp.sum(loss_rows, axis=1, keepdims=True), axis=0, keepdims=True) / img

    whole_t = tile_got.at[pl.ds(0, ncls - 1)]
    pltpu.make_async_copy(whole_t, whole_t, tile_recv).wait()
    bands = []
    for t in range(tile_rows):
        tiles = []
        for c in range(2 * tile_cols):
            index = t * tile_cols + c % tile_cols
            tiles.append(tile_got[(index // per) * 2 + c // tile_cols, index % per])
        bands.append(jnp.concatenate(tiles, axis=1))
    unit_grad = jnp.concatenate(bands, axis=0)
    exact, inverse = unit_rows(strong_own[...])
    egrad_out[...] = (unit_grad - exact * jnp.sum(exact * unit_grad, axis=1, keepdims=True)) * inverse
    for view in range(2):
        for away, k in sends:
            gather_copy(view, away, k).wait_send()
        for away in range(2):
            sent = sib_whole(view, away)
            pltpu.make_async_copy(sent, sent, sib_send.at[view, away]).wait()
    for n in range(3):
        sent = got_a.at[n, pl.ds(0, ncls - 1)]
        pltpu.make_async_copy(sent, sent, a_send.at[n]).wait()
        sent = got_b.at[n, pl.ds(0, nz - 1)]
        pltpu.make_async_copy(sent, sent, b_send.at[n]).wait()
    for part in range(2):
        half_copy(part).wait_send()
        sent = plane_got.at[part, pl.ds(0, nplane - 1)]
        pltpu.make_async_copy(sent, sent, plane_send.at[part]).wait()
    pltpu.make_async_copy(whole_z, whole_z, z_send_sem).wait()
    pltpu.make_async_copy(whole_t, whole_t, tile_send).wait()


def store(fresh_in, cgrad_in, egrad_in, loss_in, fresh_out, cgrad_out, egrad_out, loss_out, sem):
    size = cgrad_in.shape[0] // PIECES
    parts = [(cgrad_in.at[pl.ds(n * size, size)], cgrad_out.at[pl.ds(n * size, size)]) for n in range(PIECES)]
    parts += [(egrad_in, egrad_out), (fresh_in, fresh_out), (loss_in, loss_out)]
    copies = [pltpu.make_async_copy(a, b, sem.at[n]) for n, (a, b) in enumerate(parts)]
    for copy in copies:
        copy.start()
    for copy in copies:
        copy.wait()


def body(nz, ncls, weak_embed, strong_embed, centers, marginal, pseudo_label, confident):
    img, width = weak_embed.shape
    classes = centers.shape[0]
    rows = img * nz
    blocks = rows // LANES
    nplane = ncls // 2
    per = (img // 8) * (width // 2 // LANES) // nplane
    vmem = pltpu.VMEM
    dma = pltpu.SemaphoreType.DMA
    scratch = [
        vmem((img, width), BF16), vmem((img, width), BF16), vmem((2, img), jnp.int32), vmem((classes // LANES, LANES), F32),
        vmem((rows, width), BF16), vmem((rows, width), BF16), vmem((nz, 2, LANES), jnp.int32),
        vmem((1, rows), jnp.int32), vmem((1, rows), F32),
        vmem((classes, width), BF16), vmem((classes, width), BF16), vmem((width, classes), BF16),
        vmem((classes, LANES), F32), vmem((classes, LANES), F32),
        vmem((classes, rows), F32), vmem((classes, rows), F32), vmem((classes, rows), F32), vmem((classes, rows), BF16),
        vmem((1, rows), F32), vmem((1, rows), F32), vmem((1, rows), F32),
        vmem((3, blocks, LANES), F32), vmem((3, blocks, LANES), F32),
        vmem((3, ncls, blocks, LANES), F32), vmem((3, nz, blocks, LANES), F32),
        vmem((1, blocks, LANES), F32), vmem((1, blocks, LANES), F32),
        vmem((2, 2, nplane, nz // 2 * per + 1, 8, LANES), F32), vmem((2, nplane, nz // 2 * per + 1, 8, LANES), F32),
        vmem((2, nplane, nz // 2 * per + 1, 8, LANES), F32),
        vmem((nz, per + 1, 8, LANES), F32), vmem((nz, per + 1, 8, LANES), F32),
        vmem((per, 8, LANES), F32), vmem((ncls, per, 8, LANES), F32),
        dma((5,)), dma((4,)),
        dma((2, nz)), dma((2, nz)), dma((2, 2)), dma((2, 2)), dma, dma,
        dma((3,)), dma((3,)), dma((3,)), dma((3,)),
        dma((2,)), dma((2,)), dma((2,)), dma((2,)), dma, dma, dma, dma,
    ]
    hbm = pl.BlockSpec(memory_space=pl.ANY)
    local = pl.BlockSpec(memory_space=pltpu.VMEM)
    shapes = (((classes // LANES, LANES), F32), ((classes, width), BF16), ((img, width), F32), ((1, 1), F32))
    results = pl.pallas_call(
        functools.partial(kernel, nz, ncls),
        out_shape=tuple(pltpu.VMEM(*shape) for shape in shapes),
        in_specs=[hbm] * 6,
        out_specs=(local,) * 4,
        scratch_shapes=scratch,
        compiler_params=pltpu.CompilerParams(
            collective_id=0, has_side_effects=True, vmem_limit_bytes=55 * 1024 * 1024
        ),
    )(
        weak_embed, strong_embed, centers, marginal.reshape(classes // LANES, LANES),
        pseudo_label.reshape(1, img), confident.reshape(1, img),
    )
    fresh, cgrad, egrad, loss = pl.pallas_call(
        store,
        out_shape=tuple(jax.ShapeDtypeStruct(*shape) for shape in shapes),
        in_specs=[local] * 4,
        out_specs=(hbm,) * 4,
        scratch_shapes=[dma((PIECES + 3,))],
        compiler_params=pltpu.CompilerParams(vmem_limit_bytes=1024 * 1024),
    )(*results)
    return fresh.reshape(classes), cgrad, egrad, loss.reshape(())


def solution(mesh):
    placed = (
        P("dp", None),
        P("dp", None),
        P(("dp", "cls"), None),
        P(("dp", "cls")),
        P("dp"),
        P("dp"),
    )
    return jax.shard_map(
        functools.partial(body, mesh.shape["dp"], mesh.shape["cls"]),
        mesh=mesh,
        in_specs=placed,
        out_specs=(P(("dp", "cls")), P(("dp", "cls"), None), P("dp", None), P()),
        check_vma=False,
    )
```
